512 devices in a mesh: gx: 32 (over y, x_hi, core), gy: 16 (over x_lo, z).
Axes of the slice: x: 4 (x_hi: 2, x_lo: 2; x = x_hi * 2 + x_lo), y: 8, z: 8, core: 2. Of those that a mesh axis runs over, the one named last changes fastest.
Arguments:
- fine_now: float32 [3, 384, 192, 128], P(None, 'gx', 'gy'), may hold values from -6 to 6
- fine_prev: float32 [3, 384, 192, 128], P(None, 'gx', 'gy'), may hold values from -6 to 6
- fine_mu: float32 [384, 192, 128], P('gx', 'gy'), may hold values from 0.5 to 2
- fine_coef: float32 [384, 192, 128], P('gx', 'gy'), may hold values from 0.03 to 0.12
- coarse_now: float32 [3, 192, 96, 128], P(None, 'gx', 'gy'), may hold values from -6 to 6
- coarse_prev: float32 [3, 192, 96, 128], P(None, 'gx', 'gy'), may hold values from -6 to 6
- coarse_mu: float32 [192, 96, 128], P('gx', 'gy'), may hold values from 0.5 to 2
- coarse_coef: float32 [192, 96, 128], P('gx', 'gy'), may hold values from 0.03 to 0.12
- src_cell: int32 [3, 4096], replicated, may hold values from 0 to 383, as said below
- src_moment: float32 [6, 4096], P(None, ('gx', 'gy')), may hold values from -48 to 48
Outputs:
- fine_next: float32 [3, 384, 192, 128], P(None, 'gx', 'gy')
- coarse_next: float32 [3, 192, 96, 128], P(None, 'gx', 'gy')
- ghost: float32 [3, 192, 96], P(None, 'gx', 'gy')
The draws below stay inside these ranges and needn't reach their ends.
Inputs may be any that keep to these rules, and one draw needn't show every extreme that they name: `src_cell`: row 0 holds x indices below 384, row 1 y indices below 192, row 2 depth indices below 128.
All inputs are finite; a program needn't handle non-finite values.
Results may differ from the reference program's by a relative error of at most 0.00013.
Values sent between devices are 32-bit elements; how exact they have to be, the bound alone decides.
No kernel may reach another device: no remote copies, remote signals or barrier semaphores. Data moves between devices by JAX's collectives and lax.ppermute only.
A program may use at most 64 MiB of HBM per device.

```python
import math
import jax
import jax.numpy as jnp

CZ = 128
FZ = 128
ITERS = 3
NCX = 192
NCY = 96
FNX = 384
FNY = 192
SOURCES = 4096


def draw_src_cell(key, part):
    key = jax.random.fold_in(key, 7)
    first, second, third = jax.random.split(key, 3)
    along_x = jax.random.randint(first, (SOURCES,), 0, FNX)
    along_y = jax.random.randint(second, (SOURCES,), 0, FNY)
    along_z = jax.random.randint(third, (SOURCES,), 0, FZ)
    along_x = along_x.at[0].set(FNX - 1).at[1].set(0)
    along_y = along_y.at[0].set(FNY - 1).at[1].set(0)
    along_z = along_z.at[0].set(FZ - 1).at[1].set(0)
    return jnp.stack([along_x, along_y, along_z]).astype(jnp.int32)


def steps_of(rng, shape, cuts, least, high):
    factor_of = 1.0
    for position, parts in cuts:
        heights = jax.random.uniform(jax.random.fold_in(jax.random.fold_in(rng, 6), position), (parts,), jnp.float32, least / len(cuts), high / len(cuts))
        factor_of = factor_of * jnp.repeat(jnp.exp(heights), shape[position] // parts).reshape((-1,) + (1,) * (len(shape) - 1 - position))
    return factor_of


def normal_values(key, dims, spread, bound, pieces=(), kind=jnp.bfloat16):
    values = jax.random.normal(key, dims, jnp.float32) * spread
    if len(pieces) > 0:
        values = steps_of(key, dims, pieces, -0.22, 0.18) * values
    return jnp.clip(values, min=-bound, max=bound).astype(kind)


def setup_inputs(seed: int = 0) -> dict:
    splits = jax.random.split(jax.random.key(seed), 11)
    fine_now = normal_values(splits[0], (3, FNX, FNY, FZ), 1.0, 6.0, ((1, 32), (2, 16)), jnp.float32)
    fine_prev = normal_values(splits[1], (3, FNX, FNY, FZ), 1.0, 6.0, ((1, 32), (2, 16)), jnp.float32)
    fine_mu = jnp.clip(jnp.exp(math.log(2.0) - 1.3862944 * jax.random.uniform(splits[2], (FNX, FNY, FZ), jnp.float32) ** steps_of(splits[2], (FNX, FNY, FZ), ((0, 32), (1, 16)), -0.2, 0.2)), 0.5, 2.0)
    fine_coef = jnp.clip(jnp.exp(math.log(0.12) - 1.3862944 * jax.random.uniform(splits[3], (FNX, FNY, FZ), jnp.float32) ** steps_of(splits[3], (FNX, FNY, FZ), ((0, 32), (1, 16)), -0.2, 0.2)), 0.03, 0.12)
    coarse_now = normal_values(splits[4], (3, NCX, NCY, CZ), 1.0, 6.0, ((1, 32), (2, 16)), jnp.float32)
    coarse_prev = normal_values(splits[5], (3, NCX, NCY, CZ), 1.0, 6.0, ((1, 32), (2, 16)), jnp.float32)
    coarse_mu = jnp.clip(jnp.exp(math.log(2.0) - 1.3862944 * jax.random.uniform(splits[6], (NCX, NCY, CZ), jnp.float32) ** steps_of(splits[6], (NCX, NCY, CZ), ((0, 32), (1, 16)), -0.2, 0.2)), 0.5, 2.0)
    coarse_coef = jnp.clip(jnp.exp(math.log(0.12) - 1.3862944 * jax.random.uniform(splits[7], (NCX, NCY, CZ), jnp.float32) ** steps_of(splits[7], (NCX, NCY, CZ), ((0, 32), (1, 16)), -0.2, 0.2)), 0.03, 0.12)
    src_cell = draw_src_cell(jax.random.fold_in(splits[10], 71), 0)
    src_moment = normal_values(splits[9], (6, SOURCES), 8.0, 48.0, ((1, 512),), jnp.float32)
    return {"fine_now": fine_now, "fine_prev": fine_prev, "fine_mu": fine_mu, "fine_coef": fine_coef, "coarse_now": coarse_now, "coarse_prev": coarse_prev, "coarse_mu": coarse_mu, "coarse_coef": coarse_coef, "src_cell": src_cell, "src_moment": src_moment}


def prolong_last(coarse):
    count = coarse.shape[-1]
    middle = 0.5 * (coarse[..., :-1] + coarse[..., 1:])
    paired = jnp.stack([coarse[..., :-1], middle], axis=-1).reshape(coarse.shape[:-1] + (2 * (count - 1),))
    return jnp.concatenate([paired, coarse[..., -1:]], axis=-1)


def restrict_last(finer):
    count = (finer.shape[-1] - 1) // 2
    return 0.25 * finer[..., 0:2 * count:2] + 0.5 * finer[..., 1:2 * count + 1:2] + 0.25 * finer[..., 2:2 * count + 2:2]


def prolong_plane(coarse):
    along_y = prolong_last(coarse)
    return jnp.swapaxes(prolong_last(jnp.swapaxes(along_y, 1, 2)), 1, 2)


def restrict_plane(finer):
    along_y = restrict_last(finer)
    return jnp.swapaxes(restrict_last(jnp.swapaxes(along_y, 1, 2)), 1, 2)


def coupled_terms(ghost_wide):
    finer = prolong_plane(ghost_wide)
    return restrict_plane(finer[:, 1:, 1:])


def horizontal_terms(wide):
    size_x = wide.shape[1] - 4
    size_y = wide.shape[2] - 4
    rows = wide[:, :, 2:2 + size_y]
    along_x = (-rows[:, 0:size_x] + 16.0 * rows[:, 1:size_x + 1] - 30.0 * rows[:, 2:size_x + 2]
               + 16.0 * rows[:, 3:size_x + 3] - rows[:, 4:size_x + 4]) / 12.0
    cols = wide[:, 2:2 + size_x]
    along_y = (-cols[:, :, 0:size_y] + 16.0 * cols[:, :, 1:size_y + 1] - 30.0 * cols[:, :, 2:size_y + 2]
               + 16.0 * cols[:, :, 3:size_y + 3] - cols[:, :, 4:size_y + 4]) / 12.0
    return along_x + along_y


def vertical_terms(field, upper, lower):
    column = jnp.concatenate([upper[..., None], field, lower[..., None]], axis=-1)
    return column[..., :-2] - 2.0 * column[..., 1:-1] + column[..., 2:]


def source_force(cells, moments, start_x, start_y, size_x, size_y, size_z):
    force = jnp.zeros((3, size_x, size_y, size_z), moments.dtype)
    pairs = ((0, 0, 0), (0, 1, 3), (0, 2, 4), (1, 0, 3), (1, 1, 1), (1, 2, 5), (2, 0, 4), (2, 1, 5), (2, 2, 2))
    limits = (size_x, size_y, size_z)
    for component, direction, moment_row in pairs:
        for sign_value in (1, -1):
            shifted = [cells[0] - start_x, cells[1] - start_y, cells[2]]
            shifted[direction] = shifted[direction] + sign_value
            inside = jnp.ones(cells.shape[1:], bool)
            for axis_number in range(3):
                inside = inside & (shifted[axis_number] >= 0) & (shifted[axis_number] < limits[axis_number])
            places = [jnp.where(inside, shifted[axis_number], limits[axis_number]).astype(jnp.int32) for axis_number in range(3)]
            force = force.at[component, places[0], places[1], places[2]].add(
                (sign_value * 0.5) * moments[moment_row], mode="drop")
    return force


def reference(fine_now, fine_prev, fine_mu, fine_coef, coarse_now, coarse_prev, coarse_mu, coarse_coef, src_cell, src_moment):
    depth = fine_now.shape[3]
    plane_pad = ((0, 0), (1, 1), (1, 1))
    lower_plane = jnp.pad(fine_now[..., depth - 2], plane_pad)
    forcing = restrict_plane(lower_plane) + 2.0 * coarse_now[..., 0] - coarse_now[..., 1]
    inverse_diag = 1.0 / (0.6 + coarse_mu[:, :, 0])
    ghost = inverse_diag * forcing
    for sweep_index in range(ITERS):
        ghost = inverse_diag * (forcing + coupled_terms(jnp.pad(ghost, plane_pad)))
    fine_ghost = prolong_plane(jnp.pad(ghost, plane_pad))[:, 2:2 + fine_now.shape[1], 2:2 + fine_now.shape[2]]
    force = source_force(src_cell, src_moment, 0, 0, fine_now.shape[1], fine_now.shape[2], depth)
    field_pad = ((0, 0), (2, 2), (2, 2), (0, 0))
    fine_terms = horizontal_terms(jnp.pad(fine_now, field_pad)) + vertical_terms(fine_now, fine_now[..., 1], fine_ghost)
    fine_next = 2.0 * fine_now - fine_prev + fine_coef[None] * (fine_mu[None] * fine_terms + force)
    coarse_terms = horizontal_terms(jnp.pad(coarse_now, field_pad)) + vertical_terms(coarse_now, ghost, jnp.zeros_like(ghost))
    coarse_next = 2.0 * coarse_now - coarse_prev + coarse_coef[None] * (coarse_mu[None] * coarse_terms * 0.25)
    return fine_next, coarse_next, ghost
```

```python
import functools

import jax
import jax.numpy as jnp
import numpy as np
from jax import lax
from jax.experimental import pallas as pl
from jax.experimental.pallas import tpu as pltpu
from jax.sharding import PartitionSpec as P

ITERS = 3
AX = ("gx", "gy")
ROWS = 128
GROW = 108
VMEM = pltpu.VMEM
SMEM = pltpu.SMEM
F32 = jnp.float32


def vspec(n):
    return [pl.BlockSpec(memory_space=VMEM)] * n


def lane_iota(shape):
    return lax.broadcasted_iota(jnp.int32, shape, len(shape) - 1)


def row_iota(shape):
    return lax.broadcasted_iota(jnp.int32, shape, 0)


def pack_x_kernel(fine, coarse, mu, mom, half, xu, xd, own, row_out, a_s, g_s):
    lane = lane_iota((1, 128))
    acc = jnp.zeros((12, 128), F32)
    for c in range(3):
        for x in range(12):
            at = c * 16 + 3 + x // 2
            if x % 2 == 0:
                w = jnp.where(lane == at, 0.5, 0.0)
            else:
                w = jnp.where((lane == at) | (lane == at + 1), 0.25, 0.0)
            acc = acc + fine[c, x, :, 126:127] * w
    a_s[...] = jnp.zeros((24, 128), F32)
    a_s[1:13, :] = acc
    g_s[...] = jnp.zeros((16, 128), F32)
    for j in range(7):
        g_s[3 + j : 4 + j, :] = (
            0.25 * a_s[2 * j : 2 * j + 1, :]
            + 0.5 * a_s[2 * j + 1 : 2 * j + 2, :]
            + 0.25 * a_s[2 * j + 2 : 2 * j + 3, :]
        )
    b = jnp.zeros((6, 128), F32)
    for i in range(6):
        for c in range(3):
            col = 2.0 * coarse[c, i, :, 0:1] - coarse[c, i, :, 1:2]
            b = b + jnp.where(lane == c * 16 + 3 + i, col, 0.0)
        inv = 1.0 / (0.6 + mu[i, :, 0:1])
        b = b + jnp.where(lane == 48 + 3 + i, inv, 0.0)
    g_s[3:9, :] = g_s[3:9, :] + b
    g = g_s[...]
    own[...] = g
    place = lane_iota((16, 128)) % 16
    for c in range(3):
        for j in range(2):
            at = 18 * (2 * c + j)
            xu[at : at + 12, :] = fine[c, 10 + j]
            xu[at + 12 : at + 18, :] = coarse[c, 4 + j]
            xd[at : at + 12, :] = fine[c, j]
            xd[at + 12 : at + 18, :] = coarse[c, j]
    xu[GROW : GROW + 16, :] = jnp.where(place < 4, pltpu.roll(g, 128 - 6, 1), 0.0)
    xd[GROW : GROW + 16, :] = jnp.where(
        (place >= 9) & (place < 13), pltpu.roll(g, 6, 1), 0.0
    )
    for ref in (xu, xd):
        ref[GROW + 16 : ROWS, :] = jnp.zeros((ROWS - GROW - 16, 128), F32)
    lanes = lane_iota((6, 128))
    want = 8 * row_iota((6, 128)) + 64 * half[0]
    t = jnp.zeros((6, 128), F32)
    for j in range(8):
        t = t + jnp.where(lanes == want + j, mom[:, j : j + 1], 0.0)
    row_out[...] = jnp.broadcast_to(jnp.sum(t, axis=0, keepdims=True), row_out.shape)


def pack_y_kernel(fine, coarse, own, rxu, rxd, yu, yd, gx):
    g = own[...] + rxu[GROW : GROW + 16, :] + rxd[GROW : GROW + 16, :]
    gx[...] = g
    for c in range(3):
        for x in range(12):
            at = 2 * (12 * c + x)
            yu[at : at + 2, :] = fine[c, x, 10:12, :]
            yd[at : at + 2, :] = fine[c, x, 0:2, :]
        for x in range(6):
            at = 72 + 2 * (6 * c + x)
            yu[at : at + 2, :] = coarse[c, x, 4:6, :]
            yd[at : at + 2, :] = coarse[c, x, 0:2, :]
    row = row_iota((16, 128))
    yu[GROW : GROW + 16, :] = jnp.where(row < 4, pltpu.roll(g, 16 - 6, 0), 0.0)
    yd[GROW : GROW + 16, :] = jnp.where((row >= 9) & (row < 13), pltpu.roll(g, 6, 0), 0.0)
    for ref in (yu, yd):
        ref[GROW + 16 : ROWS, :] = jnp.zeros((ROWS - GROW - 16, 128), F32)


def step_kernel(
    fine, prev, mu, coef, coarse, cprev, cmu, ccoef, gx, rxu, rxd, ryu, ryd,
    base, cnext, ghost, g_s, f_s, yf, yc,
):
    lane = lane_iota((16, 128))
    g_in = gx[...] + ryu[GROW : GROW + 16, :] + ryd[GROW : GROW + 16, :]
    only = jnp.where((lane >= 48) & (lane < 64), g_in, 0.0)
    inv = pltpu.roll(only, 128 - 48, 1) + pltpu.roll(only, 128 - 32, 1) + pltpu.roll(only, 128 - 16, 1)
    g = inv * g_in
    for _ in range(ITERS):
        t = (pltpu.roll(g, 1, 1) + pltpu.roll(g, 127, 1) + 6.0 * g) * 0.125
        t = (pltpu.roll(t, 1, 0) + pltpu.roll(t, 15, 0) + 6.0 * t) * 0.125
        g = inv * (g_in + t)
    g_s[...] = g
    turned = g.T
    for c in range(3):
        ghost[c] = turned[16 * c + 3 : 16 * c + 9, 3:9]
    for j in range(6):
        low = g_s[3 + j : 4 + j, :]
        f_s[2 * j : 2 * j + 1, :] = low
        f_s[2 * j + 1 : 2 * j + 2, :] = 0.5 * (low + g_s[4 + j : 5 + j, :])
    even = f_s[...][0:12]
    odd = 0.5 * (even + pltpu.roll(even, 127, 1))
    coarse_g = g_s[3:9, :]

    lane12 = lane_iota((12, 128))
    for c in range(3):
        for x in range(12):
            k = 12 * c + x
            yf[k, 0:2, :] = ryu[2 * k : 2 * k + 2, :]
            yf[k, 2:14, :] = fine[c, x]
            yf[k, 14:16, :] = ryd[2 * k : 2 * k + 2, :]
        for x in range(6):
            k = 6 * c + x
            yc[k, 0:2, :] = ryu[72 + 2 * k : 74 + 2 * k, :]
            yc[k, 2:8, :] = coarse[c, x]
            yc[k, 8:10, :] = ryd[72 + 2 * k : 74 + 2 * k, :]

    def fine_at(c, x):
        if x < 0:
            at = 18 * (2 * c + x + 2)
            return rxu[at : at + 12, :]
        if x >= 12:
            at = 18 * (2 * c + x - 12)
            return rxd[at : at + 12, :]
        return fine[c, x]

    def coarse_at(c, x):
        if x < 0:
            at = 18 * (2 * c + x + 2) + 12
            return rxu[at : at + 6, :]
        if x >= 6:
            at = 18 * (2 * c + x - 6) + 12
            return rxd[at : at + 6, :]
        return coarse[c, x]

    for x in range(12):
        cm = coef[x] * mu[x]
        for c in range(3):
            u = fine[c, x]
            k = 12 * c + x
            near = fine_at(c, x - 1) + fine_at(c, x + 1) + yf[k, 1:13, :] + yf[k, 3:15, :]
            far = fine_at(c, x - 2) + fine_at(c, x + 2) + yf[k, 0:12, :] + yf[k, 4:16, :]
            below = pltpu.roll(u, 127, 1)
            above = jnp.where(lane12 == 0, below, pltpu.roll(u, 1, 1))
            at = 16 * c + 3 + x // 2
            edge = (even if x % 2 == 0 else odd)[:, at : at + 1]
            below = jnp.where(lane12 == 127, edge, below)
            terms = (16.0 * near - far) * (1.0 / 12.0) - 7.0 * u + above + below
            base[c, x] = 2.0 * u - prev[c, x] + cm * terms
    lane6 = lane_iota((6, 128))
    for x in range(6):
        cm = 0.25 * (ccoef[x] * cmu[x])
        for c in range(3):
            u = coarse[c, x]
            k = 6 * c + x
            near = coarse_at(c, x - 1) + coarse_at(c, x + 1) + yc[k, 1:7, :] + yc[k, 3:9, :]
            far = coarse_at(c, x - 2) + coarse_at(c, x + 2) + yc[k, 0:6, :] + yc[k, 4:10, :]
            at = 16 * c + 3 + x
            above = jnp.where(lane6 == 0, coarse_g[:, at : at + 1], pltpu.roll(u, 1, 1))
            below = jnp.where(lane6 == 127, 0.0, pltpu.roll(u, 127, 1))
            terms = (16.0 * near - far) * (1.0 / 12.0) - 7.0 * u + above + below
            cnext[c, x] = 2.0 * u - cprev[c, x] + cm * terms


K = 32


def matrices(first, second):
    device = first >> 3
    row, half = row_of(device)
    pick = jnp.where(lane_iota((K, ROWS_ALL)) == row, 1.0, 0.0)
    lanes = lane_iota((K, 128))
    base_lane = 64 * half + (first & 7)
    z = second & 127
    live = first >= 0
    here = jnp.where((lanes == z) & live, 1.0, 0.0)
    step = jnp.where((lanes == z + 1) & live, 1.0, 0.0) - jnp.where((lanes == z - 1) & live, 1.0, 0.0)
    lx = (second >> 11) - 1
    ly = ((second >> 7) & 15) - 1
    at = 16 * lx + ly
    place = lane_iota((K, 256))
    along_x = jnp.where(place == at + 16, 1.0, 0.0) - jnp.where(place == at - 16, 1.0, 0.0)
    along_y = jnp.where(place == at + 1, 1.0, 0.0) - jnp.where(place == at - 1, 1.0, 0.0)
    centre = jnp.where(place == at, 1.0, 0.0)
    spread = jnp.concatenate([along_x, along_y, centre, jnp.zeros((128 - 3 * K, 256), F32)], axis=0)
    return pick, jnp.broadcast_to(base_lane, (K, 128)), here, step, spread.T


def columns(number, rank, first, second):
    want = (row_iota((K, 128)) + number * K).astype(F32)
    one = jnp.zeros((K, 128), F32)
    two = jnp.zeros((K, 128), F32)
    for r in range(32):
        same = rank[r : r + 1, :] == want
        one = one + jnp.where(same, first[r : r + 1, :], 0.0)
        two = two + jnp.where(same, second[r : r + 1, :], 0.0)
    one = jnp.sum(one, axis=1, keepdims=True).astype(jnp.int32) - 1
    two = jnp.sum(two, axis=1, keepdims=True).astype(jnp.int32)
    return one, two


def find_kernel(start, cells, count, rank, first, second, pick, base_lane, here, step, spread, hit_s):
    lane = lane_iota((1, 128))
    for r in range(32):
        part = cells[:, 128 * r : 128 * (r + 1)]
        lx = part[0:1, :] - start[0]
        ly = part[1:2, :] - start[1]
        inside = (lx >= -1) & (lx <= 12) & (ly >= -1) & (ly <= 12)
        hit_s[r : r + 1, :] = jnp.where(inside, 1.0, 0.0)
        first[r : r + 1, :] = (lane + (128 * r + 1)).astype(F32)
        second[r : r + 1, :] = (((lx + 1) << 11) + ((ly + 1) << 7) + part[2:3, :]).astype(F32)
    hit = hit_s[...]
    square = (128, 128)
    before = jnp.where(row_iota(square) < lane_iota(square), 1.0, 0.0)
    within = jnp.dot(hit, before, preferred_element_type=F32)
    total = jnp.dot(hit, jnp.ones(square, F32), preferred_element_type=F32)
    above = jnp.where(lane_iota((32, 32)) < row_iota((32, 32)), 1.0, 0.0)
    earlier = jnp.dot(above, total, preferred_element_type=F32)
    rank[...] = jnp.where(hit > 0.0, within + earlier, -1.0)
    count[0] = jnp.sum(hit).astype(jnp.int32)
    one, two = columns(0, rank, first, second)
    pick[...], base_lane[...], here[...], step[...], spread[...] = matrices(one, two)


def source_kernel(count, rank, first, second, pick, base_lane, here, step, spread, base, coef, rows, out):
    def add(source, pick, base_lane, here, step, spread):
        line = jnp.dot(pick, rows[...], precision=lax.Precision.HIGHEST, preferred_element_type=F32)
        lanes = lane_iota((K, 128)) - base_lane
        m = [
            0.5 * jnp.sum(jnp.where(lanes == 8 * i, line, 0.0), axis=1, keepdims=True) for i in range(6)
        ]
        pad = jnp.zeros((128 - 3 * K, 128), F32)
        wide = []
        for a, b, c in ((0, 3, 4), (3, 1, 5), (4, 5, 2)):
            wide.append(jnp.concatenate([m[a] * here, m[b] * here, m[c] * step, pad], axis=0))
        wide = jnp.concatenate(wide, axis=1)
        force = jnp.dot(spread, wide, precision=lax.Precision.HIGHEST, preferred_element_type=F32)
        for x in range(12):
            for c in range(3):
                out[c, x] = source[c, x] + coef[x] * force[16 * x : 16 * x + 12, 128 * c : 128 * (c + 1)]

    add(base, pick[...], base_lane[...], here[...], step[...], spread[...])

    def more(number, carry):
        one, two = columns(number, rank, first, second)
        add(out, *matrices(one, two))
        return carry

    lax.fori_loop(1, (count[0] + K - 1) // K, more, 0)


TWO = False
IDS = np.arange(512).reshape(8, 8, 8)
STAGE1 = IDS.transpose(0, 2, 1).reshape(64, 8).tolist()
STAGE2 = IDS.transpose(1, 0, 2).reshape(8, 64).tolist()
ROWS_ALL = 256 if TWO else 512


def row_of(d):
    if not TWO:
        return d, 0
    first = (d >> 3) & 7
    second = ((d >> 6) << 3) | (d & 7)
    return second * 4 + (first >> 1), first & 1


def shape(*dims):
    return jax.ShapeDtypeStruct(dims, F32)


def shifted(x, axis, step):
    size = lax.axis_size(axis)
    pairs = [(i, i + step) for i in range(size) if 0 <= i + step < size]
    return lax.ppermute(x, axis, pairs)


def local(
    fine_now, fine_prev, fine_mu, fine_coef, coarse_now, coarse_prev, coarse_mu, coarse_coef, src_cell, src_moment,
):
    ix = lax.axis_index("gx")
    iy = lax.axis_index("gy")
    device = ix * 16 + iy
    half = (row_of(device)[1] + 0 * device).astype(jnp.int32).reshape(1)
    start = jnp.stack([ix * 12, iy * 12]).astype(jnp.int32)
    params = pltpu.CompilerParams(vmem_limit_bytes=32 * 1024 * 1024)

    xu, xd, own, row = pl.pallas_call(
        pack_x_kernel,
        in_specs=vspec(4) + [pl.BlockSpec(memory_space=SMEM)],
        out_specs=vspec(4),
        out_shape=[shape(ROWS, 128), shape(ROWS, 128), shape(16, 128), shape(8 if TWO else 512, 128)],
        scratch_shapes=[VMEM((24, 128), F32), VMEM((16, 128), F32)],
        compiler_params=params,
        name="pack_x",
    )(fine_now, coarse_now, coarse_mu, src_moment, half)
    if TWO:
        first = lax.all_to_all(row.reshape(8, 1, 128), AX, 0, 0, tiled=True, axis_index_groups=STAGE1)
    else:
        gathered = lax.all_to_all(row.reshape(512, 1, 128), AX, 0, 0, tiled=True)
    rxu = shifted(xu, "gx", 1)
    rxd = shifted(xd, "gx", -1)
    found = pl.pallas_call(
        find_kernel,
        in_specs=[pl.BlockSpec(memory_space=SMEM), pl.BlockSpec(memory_space=VMEM)],
        out_specs=[pl.BlockSpec(memory_space=SMEM)] + vspec(8),
        out_shape=[
            jax.ShapeDtypeStruct((1,), jnp.int32),
            shape(32, 128), shape(32, 128), shape(32, 128), shape(K, ROWS_ALL),
            jax.ShapeDtypeStruct((K, 128), jnp.int32),
            shape(K, 128), shape(K, 128), shape(256, 128),
        ],
        scratch_shapes=[VMEM((32, 128), F32)],
        compiler_params=params,
        name="find_sources",
    )(start, src_cell)
    yu, yd, gx = pl.pallas_call(
        pack_y_kernel,
        in_specs=vspec(5),
        out_specs=vspec(3),
        out_shape=[shape(ROWS, 128), shape(ROWS, 128), shape(16, 128)],
        compiler_params=params,
        name="pack_y",
    )(fine_now, coarse_now, own, rxu, rxd)
    ryu = shifted(yu, "gy", 1)
    ryd = shifted(yd, "gy", -1)
    if TWO:
        packed = jnp.sum(first.reshape(4, 2, 128), axis=1)
        gathered = lax.all_to_all(
            jnp.broadcast_to(packed[None], (64, 4, 128)), AX, 0, 0, tiled=True, axis_index_groups=STAGE2
        )
    base, cnext, ghost = pl.pallas_call(
        step_kernel,
        in_specs=vspec(13),
        out_specs=vspec(3),
        out_shape=[shape(3, 12, 12, 128), shape(3, 6, 6, 128), shape(3, 6, 6)],
        scratch_shapes=[
            VMEM((16, 128), F32),
            VMEM((16, 128), F32),
            VMEM((36, 16, 128), F32),
            VMEM((18, 16, 128), F32),
        ],
        compiler_params=params,
        name="step",
    )(
        fine_now, fine_prev, fine_mu, fine_coef, coarse_now, coarse_prev, coarse_mu, coarse_coef,
        gx, rxu, rxd, ryu, ryd,
    )
    fine_next = pl.pallas_call(
        source_kernel,
        in_specs=[pl.BlockSpec(memory_space=SMEM)] + vspec(11),
        out_specs=pl.BlockSpec(memory_space=VMEM),
        out_shape=shape(3, 12, 12, 128),
        compiler_params=params,
        name="add_sources",
    )(*found, base, fine_coef, gathered.reshape(ROWS_ALL, 128))
    return fine_next, cnext, ghost


def solution(mesh):
    in_specs = (
        P(None, "gx", "gy", None),
        P(None, "gx", "gy", None),
        P("gx", "gy", None),
        P("gx", "gy", None),
        P(None, "gx", "gy", None),
        P(None, "gx", "gy", None),
        P("gx", "gy", None),
        P("gx", "gy", None),
        P(),
        P(None, ("gx", "gy")),
    )
    out_specs = (P(None, "gx", "gy", None), P(None, "gx", "gy", None), P(None, "gx", "gy"))
    return jax.shard_map(local, mesh=mesh, in_specs=in_specs, out_specs=out_specs, check_vma=False)
```

```python
import jax
import jax.numpy as jnp
from jax import lax
from jax.experimental import pallas as pl
from jax.experimental.pallas import tpu as pltpu
from jax.sharding import PartitionSpec as P

ITERS = 3
NX, NY = 32, 16
FIRST_LIMIT = 60 * 1024 * 1024
AX = ("gx", "gy")
ROWS = 160
GROW = 108
ROWS_X = 160
GROW_X = 144
VMEM = pltpu.VMEM
F32 = jnp.float32


def vspec(n):
    return [pl.BlockSpec(memory_space=VMEM)] * n


def lane_iota(shape):
    return lax.broadcasted_iota(jnp.int32, shape, len(shape) - 1)


def row_iota(shape):
    return lax.broadcasted_iota(jnp.int32, shape, 0)


def interface_piece(fine, coarse, mu, a_s, g_s, ready):
    lane = lane_iota((1, 128))
    b = jnp.zeros((6, 128), F32)
    ready(3)
    ready(4)
    for i in range(6):
        for c in range(3):
            col = 2.0 * coarse[c, i, :, 0:1] - coarse[c, i, :, 1:2]
            b = b + jnp.where(lane == c * 16 + 3 + i, col, 0.0)
        inv = 1.0 / (0.6 + mu[i, :, 0:1])
        b = b + jnp.where(lane == 48 + 3 + i, inv, 0.0)
    acc = jnp.zeros((12, 128), F32)
    for c in range(3):
        ready(c)
        for x in range(12):
            at = c * 16 + 3 + x // 2
            if x % 2 == 0:
                w = jnp.where(lane == at, 0.5, 0.0)
            else:
                w = jnp.where((lane == at) | (lane == at + 1), 0.25, 0.0)
            acc = acc + fine[c, x, :, 126:127] * w
    a_s[...] = jnp.zeros((24, 128), F32)
    a_s[1:13, :] = acc
    g_s[...] = jnp.zeros((16, 128), F32)
    for j in range(7):
        g_s[3 + j : 4 + j, :] = (
            0.25 * a_s[2 * j : 2 * j + 1, :]
            + 0.5 * a_s[2 * j + 1 : 2 * j + 2, :]
            + 0.25 * a_s[2 * j + 2 : 2 * j + 3, :]
        )
    g_s[3:9, :] = g_s[3:9, :] + b


def rows_kernel(fine_hbm, coarse_hbm, mu_hbm, mom_hbm, rows, a_s, g_s, fine, coarse, mu, mom, sems):
    copies = [pltpu.make_async_copy(fine_hbm.at[c], fine.at[c], sems.at[c]) for c in range(3)]
    copies.append(pltpu.make_async_copy(coarse_hbm, coarse, sems.at[3]))
    copies.append(pltpu.make_async_copy(mu_hbm, mu, sems.at[4]))
    copies.append(pltpu.make_async_copy(mom_hbm, mom, sems.at[5]))
    for n in (5, 3, 4, 0, 1, 2):
        copies[n].start()
    lane = lane_iota((1, 128))
    lanes = lane_iota((6, 128))
    want = 8 * row_iota((6, 128)) + 64
    t = jnp.zeros((6, 128), F32)
    copies[5].wait()
    for j in range(8):
        t = t + jnp.where(lanes == want + j, mom[:, j : j + 1], 0.0)
    row = jnp.sum(t, axis=0, keepdims=True)
    rows[...] = jnp.broadcast_to(row, rows.shape)
    interface_piece(fine, coarse, mu, a_s, g_s, lambda n: copies[n].wait())
    ix = lax.axis_index("gx")
    iy = lax.axis_index("gy")
    for a in (1, -1):
        for b in (1, -1):
            from_x, from_y = 6 if a > 0 else 3, 6 if b > 0 else 3
            corner = row
            for j in range(4):
                line = pltpu.roll(g_s[from_y + j : from_y + j + 1, :], (128 + 4 * j - from_x) % 128, 1)
                corner = corner + jnp.where((lane < 64) & ((lane & 15) // 4 == j), line, 0.0)

            @pl.when(inside(ix + a, iy + b))
            def _():
                rows[pl.ds((ix + a) * NY + iy + b, 1), :] = corner


def pack_kernel(fine, coarse, mu, own, xa, xb, ya, yb, a_s, g_s):
    interface_piece(fine, coarse, mu, a_s, g_s, lambda n: None)
    g = g_s[...]
    own[...] = g
    odd_x = (lax.axis_index("gx") & 1) == 1
    odd_y = (lax.axis_index("gy") & 1) == 1

    def put(refs, odd, rows, up, down):
        one, two = refs
        one[rows, :] = jnp.where(odd, down, up)
        two[rows, :] = jnp.where(odd, up, down)

    for c in range(3):
        for j in range(2):
            at = 24 * (2 * c + j)
            put((xa, xb), odd_x, slice(at, at + 12), fine[c, 10 + j], fine[c, j])
            put((xa, xb), odd_x, slice(at + 16, at + 22), coarse[c, 4 + j], coarse[c, j])
        for x in range(12):
            at = 2 * (12 * c + x)
            put((ya, yb), odd_y, slice(at, at + 2), fine[c, x, 10:12, :], fine[c, x, 0:2, :])
        for x in range(6):
            at = 72 + 2 * (6 * c + x)
            put((ya, yb), odd_y, slice(at, at + 2), coarse[c, x, 4:6, :], coarse[c, x, 0:2, :])
    place = lane_iota((16, 128)) & 15
    row = row_iota((16, 128))
    here = slice(GROW, GROW + 16)
    up = jnp.where(place < 4, pltpu.roll(g, 128 - 6, 1), 0.0)
    down = jnp.where((place >= 9) & (place < 13), pltpu.roll(g, 6, 1), 0.0)
    put((xa, xb), odd_x, slice(GROW_X, ROWS_X), up, down)
    up = jnp.where(row < 4, pltpu.roll(g, 16 - 6, 0), 0.0)
    down = jnp.where((row >= 9) & (row < 13), pltpu.roll(g, 6, 0), 0.0)
    put((ya, yb), odd_y, here, up, down)
    for ref in (ya, yb):
        ref[GROW + 16 : ROWS, :] = jnp.zeros((ROWS - GROW - 16, 128), F32)


def inside(x, y):
    return (x >= 0) & (x < NX) & (y >= 0) & (y < NY)


def lower(rows, one, two, odd):
    return jnp.where(odd, one[rows, :], two[rows, :])


def upper(rows, one, two, odd):
    return jnp.where(odd, two[rows, :], one[rows, :])


def base_kernel(fine, prev, mu, coef, coarse, cprev, cmu, ccoef, ya, yb, base, cbase, yf, yc):
    odd_y = (lax.axis_index("gy") & 1) == 1

    def terms(field, pad, c, x, at, size, edge):
        u = field[c, x]
        k = size * c + x
        rows = slice(at + 2 * k, at + 2 * k + 2)
        pad[k, 0:2, :] = lower(rows, ya, yb, odd_y)
        pad[k, 2 : size + 2, :] = u
        pad[k, size + 2 : size + 4, :] = upper(rows, ya, yb, odd_y)
        near = pad[k, 1 : size + 1, :] + pad[k, 3 : size + 3, :]
        far = pad[k, 0:size, :] + pad[k, 4 : size + 4, :]
        for d in (-1, 1):
            if 0 <= x + d < size:
                near = near + field[c, x + d]
            if 0 <= x + 2 * d < size:
                far = far + field[c, x + 2 * d]
        below = pltpu.roll(u, 127, 1)
        above = pltpu.roll(u, 1, 1)
        lane = lane_iota((size, 128))
        above = jnp.where(lane == 0, below if edge else 0.0, above)
        below = jnp.where(lane == 127, 0.0, below)
        return u, (16.0 * near - far) * (1.0 / 12.0) - 7.0 * u + above + below

    for x in range(12):
        cm = coef[x] * mu[x]
        for c in range(3):
            u, t = terms(fine, yf, c, x, 0, 12, True)
            base[c, x] = 2.0 * u - prev[c, x] + cm * t
    for x in range(6):
        cm = 0.25 * (ccoef[x] * cmu[x])
        for c in range(3):
            u, t = terms(coarse, yc, c, x, 72, 6, False)
            cbase[c, x] = 2.0 * u - cprev[c, x] + cm * t


def finish_kernel(
    pick, rank, first, second, base_lane, here, step, spread,
    base, cbase, mu, coef, cmu, ccoef, own, ya, yb, xb, xa, rows,
    fnext, cnext, ghost, g_s, f_s, force,
):
    lane = lane_iota((16, 128))
    line = lane_iota((1, 128))
    force[...] = source_force(rows, pick[...], base_lane[...], here[...], step[...], spread[...])
    g_s[...] = own[...]
    for ref, at in ((ya, GROW), (yb, GROW), (xa, GROW_X), (xb, GROW_X)):
        g_s[...] = g_s[...] + ref[at : at + 16, :]
    ix = lax.axis_index("gx")
    iy = lax.axis_index("gy")
    for a in (1, -1):
        for b in (1, -1):
            ok = inside(ix + a, iy + b)
            at = jnp.where(ok, (ix + a) * NY + iy + b, 0)
            corner = jnp.where(ok, rows[pl.ds(at, 1), :], 0.0)
            to_x, to_y = 9 if a > 0 else 0, 9 if b > 0 else 0
            keep = (line < 64) & ((line & 15) >= to_x) & ((line & 15) < to_x + 4)
            for j in range(4):
                part = jnp.where(keep, pltpu.roll(corner, (128 + to_x - 4 * j) % 128, 1), 0.0)
                g_s[to_y + j : to_y + j + 1, :] = g_s[to_y + j : to_y + j + 1, :] + part
    g_in = g_s[...]
    only = jnp.where((lane >= 48) & (lane < 64), g_in, 0.0)
    inv = pltpu.roll(only, 128 - 48, 1) + pltpu.roll(only, 128 - 32, 1) + pltpu.roll(only, 128 - 16, 1)
    g = inv * g_in
    for _ in range(ITERS):
        t = (pltpu.roll(g, 1, 1) + pltpu.roll(g, 127, 1) + 6.0 * g) * 0.125
        t = (pltpu.roll(t, 1, 0) + pltpu.roll(t, 15, 0) + 6.0 * t) * 0.125
        g = inv * (g_in + t)
    g_s[...] = g
    turned = g.T
    for c in range(3):
        ghost[c] = turned[16 * c + 3 : 16 * c + 9, 3:9]
    for j in range(6):
        low = g_s[3 + j : 4 + j, :]
        f_s[2 * j : 2 * j + 1, :] = low
        f_s[2 * j + 1 : 2 * j + 2, :] = 0.5 * (low + g_s[4 + j : 5 + j, :])
    even = f_s[0:12, :]
    odd = 0.5 * (even + pltpu.roll(even, 127, 1))
    coarse_g = g_s[3:9, :]
    def more(number, carry):
        force[...] = force[...] + source_force(rows, *matrices(*columns(number, rank, first, second)))
        return carry

    found = jnp.max(rank[...]).astype(jnp.int32) + 1
    lax.fori_loop(1, (found + K - 1) // K, more, 0)

    odd_x = (ix & 1) == 1

    def halo(c, x, at, size):
        low = [lower(slice(n + at, n + at + size), xa, xb, odd_x) for n in (48 * c, 48 * c + 24)]
        high = [upper(slice(n + at, n + at + size), xa, xb, odd_x) for n in (48 * c, 48 * c + 24)]
        if x == 0:
            return (16.0 * low[1] - low[0]) * (1.0 / 12.0)
        if x == 1:
            return low[1] * (-1.0 / 12.0)
        if x == size - 2:
            return high[0] * (-1.0 / 12.0)
        if x == size - 1:
            return (16.0 * high[0] - high[1]) * (1.0 / 12.0)
        return 0.0

    lane12 = lane_iota((12, 128))
    for x in range(12):
        cm = coef[x] * mu[x]
        for c in range(3):
            at = 16 * c + 3 + x // 2
            edge = (even if x % 2 == 0 else odd)[:, at : at + 1]
            extra = halo(c, x, 0, 12) + jnp.where(lane12 == 127, edge, 0.0)
            push = coef[x] * force[16 * x : 16 * x + 12, 128 * c : 128 * (c + 1)]
            fnext[c, x] = base[c, x] + cm * extra + push
    lane6 = lane_iota((6, 128))
    for x in range(6):
        cm = 0.25 * (ccoef[x] * cmu[x])
        for c in range(3):
            at = 16 * c + 3 + x
            extra = halo(c, x, 16, 6) + jnp.where(lane6 == 0, coarse_g[:, at : at + 1], 0.0)
            cnext[c, x] = cbase[c, x] + cm * extra


K = 24
PART = 80


def matrices(first, second):
    lanes = lane_iota((K, 128))
    base_lane = jnp.broadcast_to(64 + (first & 7), (K, 128))
    z = second & 127
    live = first >= 0
    here = jnp.where((lanes == z) & live, 1.0, 0.0)
    step = jnp.where((lanes == z + 1) & live, 1.0, 0.0) - jnp.where((lanes == z - 1) & live, 1.0, 0.0)
    lx = (second >> 11) - 1
    ly = ((second >> 7) & 15) - 1
    at = 16 * lx + ly
    place = lane_iota((K, 192))
    along_x = jnp.where(place == at + 16, 1.0, 0.0) - jnp.where(place == at - 16, 1.0, 0.0)
    along_y = jnp.where(place == at + 1, 1.0, 0.0) - jnp.where(place == at - 1, 1.0, 0.0)
    centre = jnp.where(place == at, 1.0, 0.0)
    part = [along_x, along_y, centre, jnp.zeros((8, 192), F32)]
    spread = jnp.concatenate(part * 3 + [jnp.zeros((256 - 3 * PART, 192), F32)], axis=0)
    pick = jnp.where(lane_iota((K, NX * NY)) == first >> 3, 1.0, 0.0)
    return pick, base_lane, here, step, spread.T.astype(jnp.bfloat16)


def columns(number, rank, first, second):
    want = (row_iota((K, 128)) + number * K).astype(F32)
    one = jnp.zeros((K, 128), F32)
    two = jnp.zeros((K, 128), F32)
    for r in range(32):
        same = rank[r : r + 1, :] == want
        one = one + jnp.where(same, first[r : r + 1, :], 0.0)
        two = two + jnp.where(same, second[r : r + 1, :], 0.0)
    one = jnp.sum(one, axis=1, keepdims=True).astype(jnp.int32) - 1
    two = jnp.sum(two, axis=1, keepdims=True).astype(jnp.int32)
    return one, two


def find_kernel(cells, pick, rank, first, second, base_lane, here, step, spread, hit_s):
    lane = lane_iota((1, 128))
    for r in range(32):
        part = cells[:, 128 * r : 128 * (r + 1)]
        lx = part[0:1, :] - 12 * lax.axis_index("gx")
        ly = part[1:2, :] - 12 * lax.axis_index("gy")
        inside = (lx >= -1) & (lx <= 12) & (ly >= -1) & (ly <= 12)
        hit_s[r : r + 1, :] = jnp.where(inside, 1.0, 0.0)
        first[r : r + 1, :] = (lane + (128 * r + 1)).astype(F32)
        second[r : r + 1, :] = (((lx + 1) << 11) + ((ly + 1) << 7) + part[2:3, :]).astype(F32)
    hit = hit_s[...]
    square = (128, 128)
    before = jnp.where(row_iota(square) < lane_iota(square), 1.0, 0.0)
    within = jnp.dot(hit, before, preferred_element_type=F32)
    total = jnp.dot(hit, jnp.ones(square, F32), preferred_element_type=F32)
    above = jnp.where(lane_iota((32, 32)) < row_iota((32, 32)), 1.0, 0.0)
    earlier = jnp.dot(above, total, preferred_element_type=F32)
    rank[...] = jnp.where(hit > 0.0, within + earlier, -1.0)
    one, two = columns(0, rank, first, second)
    pick[...], base_lane[...], here[...], step[...], spread[...] = matrices(one, two)


def exact_parts(x):
    parts = []
    for _ in range(3):
        parts.append(x.astype(jnp.bfloat16))
        x = x - parts[-1].astype(F32)
    return parts


def source_force(rows, pick, base_lane, here, step, spread):
    line = jnp.dot(
        pick.astype(jnp.bfloat16), jnp.concatenate(exact_parts(rows[...]), axis=1), preferred_element_type=F32
    )
    line = line[:, 0:128] + line[:, 128:256] + line[:, 256:384]
    lanes = lane_iota((K, 128)) - base_lane
    m = [0.5 * jnp.sum(jnp.where(lanes == 8 * i, line, 0.0), axis=1, keepdims=True) for i in range(6)]
    zeros = jnp.zeros((8, 128), F32)
    wide = []
    for a, b, c in ((0, 3, 4), (3, 1, 5), (4, 5, 2)):
        wide.append(jnp.concatenate([m[a] * here, m[b] * here, m[c] * step, zeros], axis=0))
    parts = exact_parts(jnp.concatenate(wide, axis=1))
    parts.append(jnp.zeros((256 - 3 * PART, 384), jnp.bfloat16))
    return jnp.dot(spread, jnp.concatenate(parts, axis=0), preferred_element_type=F32)


def shape(*dims):
    return jax.ShapeDtypeStruct(dims, F32)


def swapped(x, axis, first):
    pairs = [(i, i + 1) for i in range(first, lax.axis_size(axis) - 1, 2)]
    return lax.ppermute(x, axis, pairs + [(j, i) for i, j in pairs])


SMALL = pltpu.CompilerParams(vmem_limit_bytes=32 * 1024 * 1024)
PIECE = [VMEM((24, 128), F32), VMEM((16, 128), F32)]


def make_rows(fine_now, coarse_now, coarse_mu, src_moment):
    return pl.pallas_call(
        rows_kernel,
        in_specs=[pl.BlockSpec(memory_space=pltpu.HBM)] * 4,
        out_specs=vspec(1)[0],
        out_shape=shape(NX * NY, 128),
        scratch_shapes=PIECE
        + [
            VMEM((3, 12, 12, 128), F32),
            VMEM((3, 6, 6, 128), F32),
            VMEM((6, 6, 128), F32),
            VMEM((6, 8), F32),
            pltpu.SemaphoreType.DMA((6,)),
        ],
        compiler_params=pltpu.CompilerParams(vmem_limit_bytes=FIRST_LIMIT),
        name="make_rows",
    )(fine_now, coarse_now, coarse_mu, src_moment)


def pack_halos(fine_now, coarse_now, coarse_mu):
    return pl.pallas_call(
        pack_kernel,
        in_specs=vspec(3),
        out_specs=vspec(5),
        out_shape=[shape(16, 128)] + [shape(ROWS_X, 128)] * 2 + [shape(ROWS, 128)] * 2,
        scratch_shapes=PIECE,
        compiler_params=SMALL,
        name="pack_halos",
    )(fine_now, coarse_now, coarse_mu)


def find_sources(src_cell):
    return pl.pallas_call(
        find_kernel,
        in_specs=vspec(1),
        out_specs=vspec(8),
        out_shape=[
            shape(K, NX * NY),
            shape(32, 128), shape(32, 128), shape(32, 128),
            jax.ShapeDtypeStruct((K, 128), jnp.int32),
            shape(K, 128), shape(K, 128), jax.ShapeDtypeStruct((192, 256), jnp.bfloat16),
        ],
        scratch_shapes=[VMEM((32, 128), F32)],
        compiler_params=SMALL,
        name="find_sources",
    )(src_cell)


def base_step(*args):
    return pl.pallas_call(
        base_kernel,
        in_specs=vspec(10),
        out_specs=vspec(2),
        out_shape=[shape(3, 12, 12, 128), shape(3, 6, 6, 128)],
        scratch_shapes=[VMEM((36, 16, 128), F32), VMEM((18, 16, 128), F32)],
        compiler_params=SMALL,
        name="base_step",
    )(*args)


def finish(*args):
    return pl.pallas_call(
        finish_kernel,
        in_specs=vspec(20),
        out_specs=vspec(3),
        out_shape=[shape(3, 12, 12, 128), shape(3, 6, 6, 128), shape(3, 6, 6)],
        scratch_shapes=[
            VMEM((16, 128), F32),
            VMEM((16, 128), F32),
            VMEM((192, 384), F32),
        ],
        compiler_params=SMALL,
        name="finish",
    )(*args)


def local(
    fine_now, fine_prev, fine_mu, fine_coef, coarse_now, coarse_prev, coarse_mu, coarse_coef, src_cell, src_moment,
):
    rows = make_rows(fine_now, coarse_now, coarse_mu, src_moment)
    gathered = lax.all_to_all(rows.reshape(NX * NY, 1, 128), AX, 0, 0, tiled=True).reshape(NX * NY, 128)
    own, xa, xb, ya, yb = pack_halos(fine_now, coarse_now, coarse_mu)
    ya, yb = swapped(ya, "gy", 0), swapped(yb, "gy", 1)
    xb, xa = swapped(xb, "gx", 1), swapped(xa, "gx", 0)
    found = find_sources(src_cell)
    base = base_step(
        fine_now, fine_prev, fine_mu, fine_coef, coarse_now, coarse_prev, coarse_mu, coarse_coef, ya, yb
    )
    return finish(
        *found, *base, fine_mu, fine_coef, coarse_mu, coarse_coef, own, ya, yb, xb, xa, gathered
    )


def solution(mesh):
    in_specs = (
        P(None, "gx", "gy", None),
        P(None, "gx", "gy", None),
        P("gx", "gy", None),
        P("gx", "gy", None),
        P(None, "gx", "gy", None),
        P(None, "gx", "gy", None),
        P("gx", "gy", None),
        P("gx", "gy", None),
        P(),
        P(None, ("gx", "gy")),
    )
    out_specs = (P(None, "gx", "gy", None), P(None, "gx", "gy", None), P(None, "gx", "gy"))
    return jax.shard_map(local, mesh=mesh, in_specs=in_specs, out_specs=out_specs, check_vma=False)
```

```python
import jax
import jax.numpy as jnp
from jax import lax
from jax.experimental import pallas as pl
from jax.experimental.pallas import tpu as pltpu
from jax.sharding import PartitionSpec as P

ITERS = 3
NX, NY = 32, 16
FIRST_LIMIT = 60 * 1024 * 1024
AX = ("gx", "gy")
ROWS_YA = 124
ROWS_YB = 136
GROW = 108
ROWS_XA = 120
ROWS_XB = 128
VMEM = pltpu.VMEM
F32 = jnp.float32


def vspec(n):
    return [pl.BlockSpec(memory_space=VMEM)] * n


def lane_iota(shape):
    return lax.broadcasted_iota(jnp.int32, shape, len(shape) - 1)


def row_iota(shape):
    return lax.broadcasted_iota(jnp.int32, shape, 0)


def interface_piece(fine, coarse, mu, a_s, g_s, ready):
    lane = lane_iota((1, 128))
    b = jnp.zeros((6, 128), F32)
    ready(3)
    ready(4)
    for i in range(6):
        for c in range(3):
            col = 2.0 * coarse[c, i, :, 0:1] - coarse[c, i, :, 1:2]
            b = b + jnp.where(lane == c * 16 + 3 + i, col, 0.0)
        inv = 1.0 / (0.6 + mu[i, :, 0:1])
        b = b + jnp.where(lane == 48 + 3 + i, inv, 0.0)
    acc = jnp.zeros((12, 128), F32)
    for c in range(3):
        ready(c)
        for x in range(12):
            at = c * 16 + 3 + x // 2
            if x % 2 == 0:
                w = jnp.where(lane == at, 0.5, 0.0)
            else:
                w = jnp.where((lane == at) | (lane == at + 1), 0.25, 0.0)
            acc = acc + fine[c, x, :, 126:127] * w
    a_s[...] = jnp.zeros((24, 128), F32)
    a_s[1:13, :] = acc
    g_s[...] = jnp.zeros((16, 128), F32)
    for j in range(7):
        g_s[3 + j : 4 + j, :] = (
            0.25 * a_s[2 * j : 2 * j + 1, :]
            + 0.5 * a_s[2 * j + 1 : 2 * j + 2, :]
            + 0.25 * a_s[2 * j + 2 : 2 * j + 3, :]
        )
    g_s[3:9, :] = g_s[3:9, :] + b


def rows_kernel(fine_hbm, coarse_hbm, mu_hbm, mom_hbm, rows, a_s, g_s, fine, coarse, mu, mom, sems):
    copies = [pltpu.make_async_copy(fine_hbm.at[c], fine.at[c], sems.at[c]) for c in range(3)]
    copies.append(pltpu.make_async_copy(coarse_hbm, coarse, sems.at[3]))
    copies.append(pltpu.make_async_copy(mu_hbm, mu, sems.at[4]))
    copies.append(pltpu.make_async_copy(mom_hbm, mom, sems.at[5]))
    for n in (5, 3, 4, 0, 1, 2):
        copies[n].start()
    lane = lane_iota((1, 128))
    lanes = lane_iota((6, 128))
    want = 8 * row_iota((6, 128)) + 64
    t = jnp.zeros((6, 128), F32)
    copies[5].wait()
    for j in range(8):
        t = t + jnp.where(lanes == want + j, mom[:, j : j + 1], 0.0)
    row = jnp.sum(t, axis=0, keepdims=True)
    rows[...] = jnp.broadcast_to(row, rows.shape)
    interface_piece(fine, coarse, mu, a_s, g_s, lambda n: copies[n].wait())
    ix = lax.axis_index("gx")
    iy = lax.axis_index("gy")
    for a in (1, -1):
        for b in (1, -1):
            from_x, from_y = 6 if a > 0 else 3, 6 if b > 0 else 3
            corner = row
            for j in range(4):
                line = pltpu.roll(g_s[from_y + j : from_y + j + 1, :], (128 + 4 * j - from_x) % 128, 1)
                corner = corner + jnp.where((lane < 64) & ((lane & 15) // 4 == j), line, 0.0)

            @pl.when(inside(ix + a, iy + b))
            def _():
                rows[pl.ds((ix + a) * NY + iy + b, 1), :] = corner


def pack_kernel(fine, coarse, mu, own, xa, xb, ya, yb, a_s, g_s):
    interface_piece(fine, coarse, mu, a_s, g_s, lambda n: None)
    g = g_s[...]
    own[...] = g
    odd_x = (lax.axis_index("gx") & 1) == 1
    odd_y = (lax.axis_index("gy") & 1) == 1

    def put(refs, odd, rows, up, down):
        one, two = refs
        one[rows, :] = jnp.where(odd, down, up)
        two[rows, :] = jnp.where(odd, up, down)

    for c in range(3):
        for j in range(2):
            at = 12 * (2 * c + j)
            put((xa, xb), odd_x, slice(at, at + 12), fine[c, 10 + j], fine[c, j])
            at = 72 + 6 * (2 * c + j)
            put((xa, xb), odd_x, slice(at, at + 6), coarse[c, 4 + j], coarse[c, j])
        for x in range(12):
            at = 2 * (12 * c + x)
            put((ya, yb), odd_y, slice(at, at + 2), fine[c, x, 10:12, :], fine[c, x, 0:2, :])
        for x in range(6):
            at = 72 + 2 * (6 * c + x)
            put((ya, yb), odd_y, slice(at, at + 2), coarse[c, x, 4:6, :], coarse[c, x, 0:2, :])
    place = lane_iota((16, 128)) & 15
    row = row_iota((16, 128))
    here = slice(GROW, GROW + 16)
    up = jnp.where(place < 4, pltpu.roll(g, 128 - 6, 1), 0.0)
    down = jnp.where((place >= 9) & (place < 13), pltpu.roll(g, 6, 1), 0.0)
    put((xa, xb), odd_x, slice(GROW, GROW + 8), up[3:11, :], down[3:11, :])
    up = jnp.where(row < 4, pltpu.roll(g, 16 - 6, 0), 0.0)
    down = jnp.where((row >= 9) & (row < 13), pltpu.roll(g, 6, 0), 0.0)
    put((ya, yb), odd_y, here, up, down)
    xa[GROW + 8 : ROWS_XA, :] = jnp.zeros((ROWS_XA - GROW - 8, 128), F32)
    yb[GROW + 16 : ROWS_YB, :] = jnp.zeros((ROWS_YB - GROW - 16, 128), F32)
    xb[GROW + 8 : ROWS_XB, :] = jnp.zeros((ROWS_XB - GROW - 8, 128), F32)


def inside(x, y):
    return (x >= 0) & (x < NX) & (y >= 0) & (y < NY)


def lower(rows, one, two, odd):
    return jnp.where(odd, one[rows, :], two[rows, :])


def upper(rows, one, two, odd):
    return jnp.where(odd, two[rows, :], one[rows, :])


def base_kernel(fine, prev, mu, coef, coarse, cprev, cmu, ccoef, ya, yb, base, cbase, yf, yc):
    odd_y = (lax.axis_index("gy") & 1) == 1

    def terms(field, pad, c, x, at, size, edge):
        u = field[c, x]
        k = size * c + x
        rows = slice(at + 2 * k, at + 2 * k + 2)
        pad[k, 0:2, :] = lower(rows, ya, yb, odd_y)
        pad[k, 2 : size + 2, :] = u
        pad[k, size + 2 : size + 4, :] = upper(rows, ya, yb, odd_y)
        near = pad[k, 1 : size + 1, :] + pad[k, 3 : size + 3, :]
        far = pad[k, 0:size, :] + pad[k, 4 : size + 4, :]
        for d in (-1, 1):
            if 0 <= x + d < size:
                near = near + field[c, x + d]
            if 0 <= x + 2 * d < size:
                far = far + field[c, x + 2 * d]
        below = pltpu.roll(u, 127, 1)
        above = pltpu.roll(u, 1, 1)
        lane = lane_iota((size, 128))
        above = jnp.where(lane == 0, below if edge else 0.0, above)
        below = jnp.where(lane == 127, 0.0, below)
        return u, (16.0 * near - far) * (1.0 / 12.0) - 7.0 * u + above + below

    for x in range(12):
        cm = coef[x] * mu[x]
        for c in range(3):
            u, t = terms(fine, yf, c, x, 0, 12, True)
            base[c, x] = 2.0 * u - prev[c, x] + cm * t
    for x in range(6):
        cm = 0.25 * (ccoef[x] * cmu[x])
        for c in range(3):
            u, t = terms(coarse, yc, c, x, 72, 6, False)
            cbase[c, x] = 2.0 * u - cprev[c, x] + cm * t


def finish_kernel(
    pick, rank, first, second, base_lane, here, step, spread,
    base, cbase, mu, coef, cmu, ccoef, own, ya, yb, xb, xa, rows,
    fnext, cnext, ghost, g_s, f_s, force,
):
    lane = lane_iota((16, 128))
    line = lane_iota((1, 128))
    force[...] = source_force(rows, pick[...], base_lane[...], here[...], step[...], spread[...])
    g_s[...] = own[...] + ya[GROW : GROW + 16, :] + yb[GROW : GROW + 16, :]
    g_s[3:11, :] = g_s[3:11, :] + xa[GROW : GROW + 8, :] + xb[GROW : GROW + 8, :]
    ix = lax.axis_index("gx")
    iy = lax.axis_index("gy")
    for a in (1, -1):
        for b in (1, -1):
            ok = inside(ix + a, iy + b)
            at = jnp.where(ok, (ix + a) * NY + iy + b, 0)
            corner = jnp.where(ok, rows[pl.ds(at, 1), :], 0.0)
            to_x, to_y = 9 if a > 0 else 0, 9 if b > 0 else 0
            keep = (line < 64) & ((line & 15) >= to_x) & ((line & 15) < to_x + 4)
            for j in range(4):
                part = jnp.where(keep, pltpu.roll(corner, (128 + to_x - 4 * j) % 128, 1), 0.0)
                g_s[to_y + j : to_y + j + 1, :] = g_s[to_y + j : to_y + j + 1, :] + part
    g_in = g_s[...]
    only = jnp.where((lane >= 48) & (lane < 64), g_in, 0.0)
    inv = pltpu.roll(only, 128 - 48, 1) + pltpu.roll(only, 128 - 32, 1) + pltpu.roll(only, 128 - 16, 1)
    g = inv * g_in
    for _ in range(ITERS):
        t = (pltpu.roll(g, 1, 1) + pltpu.roll(g, 127, 1) + 6.0 * g) * 0.125
        t = (pltpu.roll(t, 1, 0) + pltpu.roll(t, 15, 0) + 6.0 * t) * 0.125
        g = inv * (g_in + t)
    g_s[...] = g
    turned = g.T
    for c in range(3):
        ghost[c] = turned[16 * c + 3 : 16 * c + 9, 3:9]
    for j in range(6):
        low = g_s[3 + j : 4 + j, :]
        f_s[2 * j : 2 * j + 1, :] = low
        f_s[2 * j + 1 : 2 * j + 2, :] = 0.5 * (low + g_s[4 + j : 5 + j, :])
    even = f_s[0:12, :]
    odd = 0.5 * (even + pltpu.roll(even, 127, 1))
    coarse_g = g_s[3:9, :]
    def more(number, carry):
        force[...] = force[...] + source_force(rows, *matrices(*columns(number, rank, first, second)))
        return carry

    found = jnp.max(rank[...]).astype(jnp.int32) + 1
    lax.fori_loop(1, (found + K - 1) // K, more, 0)

    odd_x = (ix & 1) == 1

    def halo(c, x, at, size):
        rows = [slice(n, n + size) for n in (at + 2 * size * c, at + 2 * size * c + size)]
        low = [lower(n, xa, xb, odd_x) for n in rows]
        high = [upper(n, xa, xb, odd_x) for n in rows]
        if x == 0:
            return (16.0 * low[1] - low[0]) * (1.0 / 12.0)
        if x == 1:
            return low[1] * (-1.0 / 12.0)
        if x == size - 2:
            return high[0] * (-1.0 / 12.0)
        if x == size - 1:
            return (16.0 * high[0] - high[1]) * (1.0 / 12.0)
        return 0.0

    lane12 = lane_iota((12, 128))
    for x in range(12):
        cm = coef[x] * mu[x]
        for c in range(3):
            at = 16 * c + 3 + x // 2
            edge = (even if x % 2 == 0 else odd)[:, at : at + 1]
            extra = halo(c, x, 0, 12) + jnp.where(lane12 == 127, edge, 0.0)
            push = coef[x] * force[16 * x : 16 * x + 12, 128 * c : 128 * (c + 1)]
            fnext[c, x] = base[c, x] + cm * extra + push
    lane6 = lane_iota((6, 128))
    for x in range(6):
        cm = 0.25 * (ccoef[x] * cmu[x])
        for c in range(3):
            at = 16 * c + 3 + x
            extra = halo(c, x, 72, 6) + jnp.where(lane6 == 0, coarse_g[:, at : at + 1], 0.0)
            cnext[c, x] = cbase[c, x] + cm * extra


K = 24
PART = 80


def matrices(first, second):
    lanes = lane_iota((K, 128))
    base_lane = jnp.broadcast_to(64 + (first & 7), (K, 128))
    z = second & 127
    live = first >= 0
    here = jnp.where((lanes == z) & live, 1.0, 0.0)
    step = jnp.where((lanes == z + 1) & live, 1.0, 0.0) - jnp.where((lanes == z - 1) & live, 1.0, 0.0)
    lx = (second >> 11) - 1
    ly = ((second >> 7) & 15) - 1
    at = 16 * lx + ly
    place = lane_iota((K, 192))
    along_x = jnp.where(place == at + 16, 1.0, 0.0) - jnp.where(place == at - 16, 1.0, 0.0)
    along_y = jnp.where(place == at + 1, 1.0, 0.0) - jnp.where(place == at - 1, 1.0, 0.0)
    centre = jnp.where(place == at, 1.0, 0.0)
    part = [along_x, along_y, centre, jnp.zeros((8, 192), F32)]
    spread = jnp.concatenate(part * 3 + [jnp.zeros((256 - 3 * PART, 192), F32)], axis=0)
    pick = jnp.where(lane_iota((K, NX * NY)) == first >> 3, 1.0, 0.0)
    return pick, base_lane, here, step, spread.T.astype(jnp.bfloat16)


def columns(number, rank, first, second):
    want = (row_iota((K, 128)) + number * K).astype(F32)
    one = jnp.zeros((K, 128), F32)
    two = jnp.zeros((K, 128), F32)
    for r in range(32):
        same = rank[r : r + 1, :] == want
        one = one + jnp.where(same, first[r : r + 1, :], 0.0)
        two = two + jnp.where(same, second[r : r + 1, :], 0.0)
    one = jnp.sum(one, axis=1, keepdims=True).astype(jnp.int32) - 1
    two = jnp.sum(two, axis=1, keepdims=True).astype(jnp.int32)
    return one, two


def find_kernel(cells, pick, rank, first, second, base_lane, here, step, spread, hit_s):
    lane = lane_iota((1, 128))
    for r in range(32):
        part = cells[:, 128 * r : 128 * (r + 1)]
        lx = part[0:1, :] - 12 * lax.axis_index("gx")
        ly = part[1:2, :] - 12 * lax.axis_index("gy")
        inside = (lx >= -1) & (lx <= 12) & (ly >= -1) & (ly <= 12)
        hit_s[r : r + 1, :] = jnp.where(inside, 1.0, 0.0)
        first[r : r + 1, :] = (lane + (128 * r + 1)).astype(F32)
        second[r : r + 1, :] = (((lx + 1) << 11) + ((ly + 1) << 7) + part[2:3, :]).astype(F32)
    hit = hit_s[...]
    square = (128, 128)
    before = jnp.where(row_iota(square) < lane_iota(square), 1.0, 0.0)
    within = jnp.dot(hit, before, preferred_element_type=F32)
    total = jnp.dot(hit, jnp.ones(square, F32), preferred_element_type=F32)
    above = jnp.where(lane_iota((32, 32)) < row_iota((32, 32)), 1.0, 0.0)
    earlier = jnp.dot(above, total, preferred_element_type=F32)
    rank[...] = jnp.where(hit > 0.0, within + earlier, -1.0)
    one, two = columns(0, rank, first, second)
    pick[...], base_lane[...], here[...], step[...], spread[...] = matrices(one, two)


def exact_parts(x):
    parts = []
    for _ in range(3):
        parts.append(x.astype(jnp.bfloat16))
        x = x - parts[-1].astype(F32)
    return parts


def source_force(rows, pick, base_lane, here, step, spread):
    line = jnp.dot(
        pick.astype(jnp.bfloat16), jnp.concatenate(exact_parts(rows[...]), axis=1), preferred_element_type=F32
    )
    line = line[:, 0:128] + line[:, 128:256] + line[:, 256:384]
    lanes = lane_iota((K, 128)) - base_lane
    m = [0.5 * jnp.sum(jnp.where(lanes == 8 * i, line, 0.0), axis=1, keepdims=True) for i in range(6)]
    zeros = jnp.zeros((8, 128), F32)
    wide = []
    for a, b, c in ((0, 3, 4), (3, 1, 5), (4, 5, 2)):
        wide.append(jnp.concatenate([m[a] * here, m[b] * here, m[c] * step, zeros], axis=0))
    parts = exact_parts(jnp.concatenate(wide, axis=1))
    parts.append(jnp.zeros((256 - 3 * PART, 384), jnp.bfloat16))
    return jnp.dot(spread, jnp.concatenate(parts, axis=0), preferred_element_type=F32)


def shape(*dims):
    return jax.ShapeDtypeStruct(dims, F32)


def swapped(x, axis, first):
    pairs = [(i, i + 1) for i in range(first, lax.axis_size(axis) - 1, 2)]
    return lax.ppermute(x, axis, pairs + [(j, i) for i, j in pairs])


SMALL = pltpu.CompilerParams(vmem_limit_bytes=32 * 1024 * 1024)
PIECE = [VMEM((24, 128), F32), VMEM((16, 128), F32)]


def make_rows(fine_now, coarse_now, coarse_mu, src_moment):
    return pl.pallas_call(
        rows_kernel,
        in_specs=[pl.BlockSpec(memory_space=pltpu.HBM)] * 4,
        out_specs=vspec(1)[0],
        out_shape=shape(NX * NY, 128),
        scratch_shapes=PIECE
        + [
            VMEM((3, 12, 12, 128), F32),
            VMEM((3, 6, 6, 128), F32),
            VMEM((6, 6, 128), F32),
            VMEM((6, 8), F32),
            pltpu.SemaphoreType.DMA((6,)),
        ],
        compiler_params=pltpu.CompilerParams(vmem_limit_bytes=FIRST_LIMIT),
        name="make_rows",
    )(fine_now, coarse_now, coarse_mu, src_moment)


def pack_halos(fine_now, coarse_now, coarse_mu):
    return pl.pallas_call(
        pack_kernel,
        in_specs=vspec(3),
        out_specs=vspec(5),
        out_shape=[shape(16, 128)] + [shape(n, 128) for n in (ROWS_XA, ROWS_XB, ROWS_YA, ROWS_YB)],
        scratch_shapes=PIECE,
        compiler_params=SMALL,
        name="pack_halos",
    )(fine_now, coarse_now, coarse_mu)


def find_sources(src_cell):
    return pl.pallas_call(
        find_kernel,
        in_specs=vspec(1),
        out_specs=vspec(8),
        out_shape=[
            shape(K, NX * NY),
            shape(32, 128), shape(32, 128), shape(32, 128),
            jax.ShapeDtypeStruct((K, 128), jnp.int32),
            shape(K, 128), shape(K, 128), jax.ShapeDtypeStruct((192, 256), jnp.bfloat16),
        ],
        scratch_shapes=[VMEM((32, 128), F32)],
        compiler_params=SMALL,
        name="find_sources",
    )(src_cell)


def base_step(*args):
    return pl.pallas_call(
        base_kernel,
        in_specs=vspec(10),
        out_specs=vspec(2),
        out_shape=[shape(3, 12, 12, 128), shape(3, 6, 6, 128)],
        scratch_shapes=[VMEM((36, 16, 128), F32), VMEM((18, 16, 128), F32)],
        compiler_params=SMALL,
        name="base_step",
    )(*args)


def finish(*args):
    return pl.pallas_call(
        finish_kernel,
        in_specs=vspec(20),
        out_specs=vspec(3),
        out_shape=[shape(3, 12, 12, 128), shape(3, 6, 6, 128), shape(3, 6, 6)],
        scratch_shapes=[
            VMEM((16, 128), F32),
            VMEM((16, 128), F32),
            VMEM((192, 384), F32),
        ],
        compiler_params=SMALL,
        name="finish",
    )(*args)


def local(
    fine_now, fine_prev, fine_mu, fine_coef, coarse_now, coarse_prev, coarse_mu, coarse_coef, src_cell, src_moment,
):
    rows = make_rows(fine_now, coarse_now, coarse_mu, src_moment)
    gathered = lax.all_to_all(rows.reshape(NX * NY, 1, 128), AX, 0, 0, tiled=True).reshape(NX * NY, 128)
    own, xa, xb, ya, yb = pack_halos(fine_now, coarse_now, coarse_mu)
    ya, yb = swapped(ya, "gy", 0), swapped(yb, "gy", 1)
    xb, xa = swapped(xb, "gx", 1), swapped(xa, "gx", 0)
    found = find_sources(src_cell)
    base = base_step(
        fine_now, fine_prev, fine_mu, fine_coef, coarse_now, coarse_prev, coarse_mu, coarse_coef, ya, yb
    )
    return finish(
        *found, *base, fine_mu, fine_coef, coarse_mu, coarse_coef, own, ya, yb, xb, xa, gathered
    )


def solution(mesh):
    in_specs = (
        P(None, "gx", "gy", None),
        P(None, "gx", "gy", None),
        P("gx", "gy", None),
        P("gx", "gy", None),
        P(None, "gx", "gy", None),
        P(None, "gx", "gy", None),
        P("gx", "gy", None),
        P("gx", "gy", None),
        P(),
        P(None, ("gx", "gy")),
    )
    out_specs = (P(None, "gx", "gy", None), P(None, "gx", "gy", None), P(None, "gx", "gy"))
    return jax.shard_map(local, mesh=mesh, in_specs=in_specs, out_specs=out_specs, check_vma=False)
```

```python
import jax
import jax.numpy as jnp
from jax import lax
from jax.experimental import pallas as pl
from jax.experimental.pallas import tpu as pltpu
from jax.sharding import PartitionSpec as P

ITERS = 3
NX, NY = 32, 16
FIRST_LIMIT = 60 * 1024 * 1024
AX = ("gx", "gy")
ROWS_YA = 124
ROWS_YB = 136
GROW = 108
ROWS_XA = 120
ROWS_XB = 128
VMEM = pltpu.VMEM
F32 = jnp.float32


def vspec(n):
    return [pl.BlockSpec(memory_space=VMEM)] * n


def lane_iota(shape):
    return lax.broadcasted_iota(jnp.int32, shape, len(shape) - 1)


def row_iota(shape):
    return lax.broadcasted_iota(jnp.int32, shape, 0)


def interface_piece(fine, coarse, mu, a_s, g_s, ready):
    lane = lane_iota((1, 128))
    b = jnp.zeros((6, 128), F32)
    ready(3)
    ready(4)
    for i in range(6):
        for c in range(3):
            col = 2.0 * coarse[c, i, :, 0:1] - coarse[c, i, :, 1:2]
            b = b + jnp.where(lane == c * 16 + 3 + i, col, 0.0)
        inv = 1.0 / (0.6 + mu[i, :, 0:1])
        b = b + jnp.where(lane == 48 + 3 + i, inv, 0.0)
    acc = jnp.zeros((12, 128), F32)
    for c in range(3):
        ready(c)
        for x in range(12):
            at = c * 16 + 3 + x // 2
            if x % 2 == 0:
                w = jnp.where(lane == at, 0.5, 0.0)
            else:
                w = jnp.where((lane == at) | (lane == at + 1), 0.25, 0.0)
            acc = acc + fine[c, x, :, 126:127] * w
    a_s[...] = jnp.zeros((24, 128), F32)
    a_s[1:13, :] = acc
    g_s[...] = jnp.zeros((16, 128), F32)
    for j in range(7):
        g_s[3 + j : 4 + j, :] = (
            0.25 * a_s[2 * j : 2 * j + 1, :]
            + 0.5 * a_s[2 * j + 1 : 2 * j + 2, :]
            + 0.25 * a_s[2 * j + 2 : 2 * j + 3, :]
        )
    g_s[3:9, :] = g_s[3:9, :] + b


def rows_kernel(fine_hbm, coarse_hbm, mu_hbm, mom_hbm, rows, a_s, g_s, fine, coarse, mu, mom, sems):
    copies = [pltpu.make_async_copy(fine_hbm.at[c], fine.at[c], sems.at[c]) for c in range(3)]
    copies.append(pltpu.make_async_copy(coarse_hbm, coarse, sems.at[3]))
    copies.append(pltpu.make_async_copy(mu_hbm, mu, sems.at[4]))
    copies.append(pltpu.make_async_copy(mom_hbm, mom, sems.at[5]))
    for n in (5, 3, 4, 0, 1, 2):
        copies[n].start()
    lane = lane_iota((1, 128))
    lanes = lane_iota((6, 128))
    want = 8 * row_iota((6, 128)) + 64
    t = jnp.zeros((6, 128), F32)
    copies[5].wait()
    for j in range(8):
        t = t + jnp.where(lanes == want + j, mom[:, j : j + 1], 0.0)
    row = jnp.sum(t, axis=0, keepdims=True)
    rows[...] = jnp.broadcast_to(row, rows.shape)
    interface_piece(fine, coarse, mu, a_s, g_s, lambda n: copies[n].wait())
    ix = lax.axis_index("gx")
    iy = lax.axis_index("gy")
    for a in (1, -1):
        for b in (1, -1):
            from_x, from_y = 6 if a > 0 else 3, 6 if b > 0 else 3
            corner = row
            for j in range(4):
                line = pltpu.roll(g_s[from_y + j : from_y + j + 1, :], (128 + 4 * j - from_x) % 128, 1)
                corner = corner + jnp.where((lane < 64) & ((lane & 15) // 4 == j), line, 0.0)

            @pl.when(inside(ix + a, iy + b))
            def _():
                rows[pl.ds((ix + a) * NY + iy + b, 1), :] = corner


def pack_kernel(fine, coarse, mu, own, xa, xb, ya, yb, a_s, g_s):
    interface_piece(fine, coarse, mu, a_s, g_s, lambda n: None)
    g = g_s[...]
    own[...] = g
    odd_x = (lax.axis_index("gx") & 1) == 1
    odd_y = (lax.axis_index("gy") & 1) == 1

    def put(refs, odd, rows, up, down):
        one, two = refs
        one[rows, :] = jnp.where(odd, down, up)
        two[rows, :] = jnp.where(odd, up, down)

    for c in range(3):
        for j in range(2):
            at = 12 * (2 * c + j)
            put((xa, xb), odd_x, slice(at, at + 12), fine[c, 10 + j], fine[c, j])
            at = 72 + 6 * (2 * c + j)
            put((xa, xb), odd_x, slice(at, at + 6), coarse[c, 4 + j], coarse[c, j])
        for x in range(12):
            at = 2 * (12 * c + x)
            put((ya, yb), odd_y, slice(at, at + 2), fine[c, x, 10:12, :], fine[c, x, 0:2, :])
        for x in range(6):
            at = 72 + 2 * (6 * c + x)
            put((ya, yb), odd_y, slice(at, at + 2), coarse[c, x, 4:6, :], coarse[c, x, 0:2, :])
    place = lane_iota((16, 128)) & 15
    row = row_iota((16, 128))
    here = slice(GROW, GROW + 16)
    up = jnp.where(place < 4, pltpu.roll(g, 128 - 6, 1), 0.0)
    down = jnp.where((place >= 9) & (place < 13), pltpu.roll(g, 6, 1), 0.0)
    put((xa, xb), odd_x, slice(GROW, GROW + 8), up[3:11, :], down[3:11, :])
    up = jnp.where(row < 4, pltpu.roll(g, 16 - 6, 0), 0.0)
    down = jnp.where((row >= 9) & (row < 13), pltpu.roll(g, 6, 0), 0.0)
    put((ya, yb), odd_y, here, up, down)
    xa[GROW + 8 : ROWS_XA, :] = jnp.zeros((ROWS_XA - GROW - 8, 128), F32)
    yb[GROW + 16 : ROWS_YB, :] = jnp.zeros((ROWS_YB - GROW - 16, 128), F32)
    xb[GROW + 8 : ROWS_XB, :] = jnp.zeros((ROWS_XB - GROW - 8, 128), F32)


def inside(x, y):
    return (x >= 0) & (x < NX) & (y >= 0) & (y < NY)


def lower(rows, one, two, odd):
    return jnp.where(odd, one[rows, :], two[rows, :])


def upper(rows, one, two, odd):
    return jnp.where(odd, two[rows, :], one[rows, :])


def base_kernel(fine, prev, mu, coef, coarse, cprev, cmu, ccoef, ya, yb, base, cbase, yf, yc):
    odd_y = (lax.axis_index("gy") & 1) == 1

    def terms(field, pad, c, x, at, size, edge):
        u = field[c, x]
        k = size * c + x
        rows = slice(at + 2 * k, at + 2 * k + 2)
        pad[k, 0:2, :] = lower(rows, ya, yb, odd_y)
        pad[k, 2 : size + 2, :] = u
        pad[k, size + 2 : size + 4, :] = upper(rows, ya, yb, odd_y)
        near = pad[k, 1 : size + 1, :] + pad[k, 3 : size + 3, :]
        far = pad[k, 0:size, :] + pad[k, 4 : size + 4, :]
        for d in (-1, 1):
            if 0 <= x + d < size:
                near = near + field[c, x + d]
            if 0 <= x + 2 * d < size:
                far = far + field[c, x + 2 * d]
        below = pltpu.roll(u, 127, 1)
        above = pltpu.roll(u, 1, 1)
        lane = lane_iota((size, 128))
        above = jnp.where(lane == 0, below if edge else 0.0, above)
        below = jnp.where(lane == 127, 0.0, below)
        return u, (16.0 * near - far) * (1.0 / 12.0) - 7.0 * u + above + below

    for x in range(12):
        cm = coef[x] * mu[x]
        for c in range(3):
            u, t = terms(fine, yf, c, x, 0, 12, True)
            base[c, x] = 2.0 * u - prev[c, x] + cm * t
    for x in range(6):
        cm = 0.25 * (ccoef[x] * cmu[x])
        for c in range(3):
            u, t = terms(coarse, yc, c, x, 72, 6, False)
            cbase[c, x] = 2.0 * u - cprev[c, x] + cm * t


def finish_kernel(
    pick, rank, first, second, base_lane, here, step, spread,
    base, cbase, mu, coef, cmu, ccoef, own, ya, yb, xb, xa, rows,
    fnext, cnext, ghost, g_s, f_s, force,
):
    lane = lane_iota((16, 128))
    line = lane_iota((1, 128))
    force[...] = source_force(rows, pick[...], base_lane[...], here[...], step[...], spread[...])
    g_s[...] = own[...] + ya[GROW : GROW + 16, :] + yb[GROW : GROW + 16, :]
    g_s[3:11, :] = g_s[3:11, :] + xa[GROW : GROW + 8, :] + xb[GROW : GROW + 8, :]
    ix = lax.axis_index("gx")
    iy = lax.axis_index("gy")
    for a in (1, -1):
        for b in (1, -1):
            ok = inside(ix + a, iy + b)
            at = jnp.where(ok, (ix + a) * NY + iy + b, 0)
            corner = jnp.where(ok, rows[pl.ds(at, 1), :], 0.0)
            to_x, to_y = 9 if a > 0 else 0, 9 if b > 0 else 0
            keep = (line < 64) & ((line & 15) >= to_x) & ((line & 15) < to_x + 4)
            for j in range(4):
                part = jnp.where(keep, pltpu.roll(corner, (128 + to_x - 4 * j) % 128, 1), 0.0)
                g_s[to_y + j : to_y + j + 1, :] = g_s[to_y + j : to_y + j + 1, :] + part
    g_in = g_s[...]
    only = jnp.where((lane >= 48) & (lane < 64), g_in, 0.0)
    inv = pltpu.roll(only, 128 - 48, 1) + pltpu.roll(only, 128 - 32, 1) + pltpu.roll(only, 128 - 16, 1)
    g = inv * g_in
    for _ in range(ITERS):
        t = (pltpu.roll(g, 1, 1) + pltpu.roll(g, 127, 1) + 6.0 * g) * 0.125
        t = (pltpu.roll(t, 1, 0) + pltpu.roll(t, 15, 0) + 6.0 * t) * 0.125
        g = inv * (g_in + t)
    g_s[...] = g
    turned = g.T
    for c in range(3):
        ghost[c] = turned[16 * c + 3 : 16 * c + 9, 3:9]
    for j in range(6):
        low = g_s[3 + j : 4 + j, :]
        f_s[2 * j : 2 * j + 1, :] = low
        f_s[2 * j + 1 : 2 * j + 2, :] = 0.5 * (low + g_s[4 + j : 5 + j, :])
    even = f_s[0:12, :]
    odd = 0.5 * (even + pltpu.roll(even, 127, 1))
    coarse_g = g_s[3:9, :]
    def more(number, carry):
        force[...] = force[...] + source_force(rows, *matrices(*columns(number, rank, first, second)))
        return carry

    found = jnp.max(rank[...]).astype(jnp.int32) + 1
    lax.fori_loop(1, (found + K - 1) // K, more, 0)

    odd_x = (ix & 1) == 1

    def halo(c, x, at, size):
        rows = [slice(n, n + size) for n in (at + 2 * size * c, at + 2 * size * c + size)]
        low = [lower(n, xa, xb, odd_x) for n in rows]
        high = [upper(n, xa, xb, odd_x) for n in rows]
        if x == 0:
            return (16.0 * low[1] - low[0]) * (1.0 / 12.0)
        if x == 1:
            return low[1] * (-1.0 / 12.0)
        if x == size - 2:
            return high[0] * (-1.0 / 12.0)
        if x == size - 1:
            return (16.0 * high[0] - high[1]) * (1.0 / 12.0)
        return 0.0

    lane12 = lane_iota((12, 128))
    for x in range(12):
        cm = coef[x] * mu[x]
        for c in range(3):
            at = 16 * c + 3 + x // 2
            edge = (even if x % 2 == 0 else odd)[:, at : at + 1]
            extra = halo(c, x, 0, 12) + jnp.where(lane12 == 127, edge, 0.0)
            push = coef[x] * force[16 * x : 16 * x + 12, 128 * c : 128 * (c + 1)]
            fnext[c, x] = base[c, x] + cm * extra + push
    lane6 = lane_iota((6, 128))
    for x in range(6):
        cm = 0.25 * (ccoef[x] * cmu[x])
        for c in range(3):
            at = 16 * c + 3 + x
            extra = halo(c, x, 72, 6) + jnp.where(lane6 == 0, coarse_g[:, at : at + 1], 0.0)
            cnext[c, x] = cbase[c, x] + cm * extra


K = 24
PART = 80


def matrices(first, second):
    lanes = lane_iota((K, 128))
    base_lane = jnp.broadcast_to(64 + (first & 7), (K, 128))
    z = second & 127
    live = first >= 0
    here = jnp.where((lanes == z) & live, 1.0, 0.0)
    step = jnp.where((lanes == z + 1) & live, 1.0, 0.0) - jnp.where((lanes == z - 1) & live, 1.0, 0.0)
    lx = (second >> 11) - 1
    ly = ((second >> 7) & 15) - 1
    at = 16 * lx + ly
    place = lane_iota((K, 192))
    along_x = jnp.where(place == at + 16, 1.0, 0.0) - jnp.where(place == at - 16, 1.0, 0.0)
    along_y = jnp.where(place == at + 1, 1.0, 0.0) - jnp.where(place == at - 1, 1.0, 0.0)
    centre = jnp.where(place == at, 1.0, 0.0)
    part = [along_x, along_y, centre, jnp.zeros((8, 192), F32)]
    spread = jnp.concatenate(part * 3 + [jnp.zeros((256 - 3 * PART, 192), F32)], axis=0)
    pick = jnp.where(lane_iota((K, NX * NY)) == first >> 3, 1.0, 0.0)
    return pick, base_lane, here, step, spread.T.astype(jnp.bfloat16)


def columns(number, rank, first, second):
    want = (row_iota((K, 128)) + number * K).astype(F32)
    one = jnp.zeros((K, 128), F32)
    two = jnp.zeros((K, 128), F32)
    for r in range(32):
        same = rank[r : r + 1, :] == want
        one = one + jnp.where(same, first[r : r + 1, :], 0.0)
        two = two + jnp.where(same, second[r : r + 1, :], 0.0)
    one = jnp.sum(one, axis=1, keepdims=True).astype(jnp.int32) - 1
    two = jnp.sum(two, axis=1, keepdims=True).astype(jnp.int32)
    return one, two


def find_kernel(cells, pick, rank, first, second, base_lane, here, step, spread, cell_s):
    for r in range(32):
        for n in range(3):
            cell_s[n, r : r + 1, :] = cells[n : n + 1, 128 * r : 128 * (r + 1)]
    lx = cell_s[0] - 12 * lax.axis_index("gx")
    ly = cell_s[1] - 12 * lax.axis_index("gy")
    hit = jnp.where((lx >= -1) & (lx <= 12) & (ly >= -1) & (ly <= 12), 1.0, 0.0)
    block = (32, 128)
    first[...] = (lane_iota(block) + 128 * row_iota(block) + 1).astype(F32)
    second[...] = (((lx + 1) << 11) + ((ly + 1) << 7) + cell_s[2]).astype(F32)
    square = (128, 128)
    before = jnp.where(row_iota(square) < lane_iota(square), 1.0, 0.0)
    within = jnp.dot(hit, before, preferred_element_type=F32)
    total = jnp.dot(hit, jnp.ones(square, F32), preferred_element_type=F32)
    above = jnp.where(lane_iota((32, 32)) < row_iota((32, 32)), 1.0, 0.0)
    earlier = jnp.dot(above, total, preferred_element_type=F32)
    rank[...] = jnp.where(hit > 0.0, within + earlier, -1.0)
    one, two = columns(0, rank, first, second)
    pick[...], base_lane[...], here[...], step[...], spread[...] = matrices(one, two)


def exact_parts(x):
    parts = []
    for _ in range(3):
        parts.append(x.astype(jnp.bfloat16))
        x = x - parts[-1].astype(F32)
    return parts


def source_force(rows, pick, base_lane, here, step, spread):
    line = jnp.dot(
        pick.astype(jnp.bfloat16), jnp.concatenate(exact_parts(rows[...]), axis=1), preferred_element_type=F32
    )
    line = line[:, 0:128] + line[:, 128:256] + line[:, 256:384]
    lanes = lane_iota((K, 128)) - base_lane
    m = [0.5 * jnp.sum(jnp.where(lanes == 8 * i, line, 0.0), axis=1, keepdims=True) for i in range(6)]
    zeros = jnp.zeros((8, 128), F32)
    wide = []
    for a, b, c in ((0, 3, 4), (3, 1, 5), (4, 5, 2)):
        wide.append(jnp.concatenate([m[a] * here, m[b] * here, m[c] * step, zeros], axis=0))
    parts = exact_parts(jnp.concatenate(wide, axis=1))
    parts.append(jnp.zeros((256 - 3 * PART, 384), jnp.bfloat16))
    return jnp.dot(spread, jnp.concatenate(parts, axis=0), preferred_element_type=F32)


def shape(*dims):
    return jax.ShapeDtypeStruct(dims, F32)


def swapped(x, axis, first):
    pairs = [(i, i + 1) for i in range(first, lax.axis_size(axis) - 1, 2)]
    return lax.ppermute(x, axis, pairs + [(j, i) for i, j in pairs])


SMALL = pltpu.CompilerParams(vmem_limit_bytes=32 * 1024 * 1024)
PIECE = [VMEM((24, 128), F32), VMEM((16, 128), F32)]


def make_rows(fine_now, coarse_now, coarse_mu, src_moment):
    return pl.pallas_call(
        rows_kernel,
        in_specs=[pl.BlockSpec(memory_space=pltpu.HBM)] * 4,
        out_specs=vspec(1)[0],
        out_shape=shape(NX * NY, 128),
        scratch_shapes=PIECE
        + [
            VMEM((3, 12, 12, 128), F32),
            VMEM((3, 6, 6, 128), F32),
            VMEM((6, 6, 128), F32),
            VMEM((6, 8), F32),
            pltpu.SemaphoreType.DMA((6,)),
        ],
        compiler_params=pltpu.CompilerParams(vmem_limit_bytes=FIRST_LIMIT),
        name="make_rows",
    )(fine_now, coarse_now, coarse_mu, src_moment)


def pack_halos(fine_now, coarse_now, coarse_mu):
    return pl.pallas_call(
        pack_kernel,
        in_specs=vspec(3),
        out_specs=vspec(5),
        out_shape=[shape(16, 128)] + [shape(n, 128) for n in (ROWS_XA, ROWS_XB, ROWS_YA, ROWS_YB)],
        scratch_shapes=PIECE,
        compiler_params=SMALL,
        name="pack_halos",
    )(fine_now, coarse_now, coarse_mu)


def find_sources(src_cell):
    return pl.pallas_call(
        find_kernel,
        in_specs=vspec(1),
        out_specs=vspec(8),
        out_shape=[
            shape(K, NX * NY),
            shape(32, 128), shape(32, 128), shape(32, 128),
            jax.ShapeDtypeStruct((K, 128), jnp.int32),
            shape(K, 128), shape(K, 128), jax.ShapeDtypeStruct((192, 256), jnp.bfloat16),
        ],
        scratch_shapes=[VMEM((3, 32, 128), jnp.int32)],
        compiler_params=SMALL,
        name="find_sources",
    )(src_cell)


def base_step(*args):
    return pl.pallas_call(
        base_kernel,
        in_specs=vspec(10),
        out_specs=vspec(2),
        out_shape=[shape(3, 12, 12, 128), shape(3, 6, 6, 128)],
        scratch_shapes=[VMEM((36, 16, 128), F32), VMEM((18, 16, 128), F32)],
        compiler_params=SMALL,
        name="base_step",
    )(*args)


def finish(*args):
    return pl.pallas_call(
        finish_kernel,
        in_specs=vspec(20),
        out_specs=vspec(3),
        out_shape=[shape(3, 12, 12, 128), shape(3, 6, 6, 128), shape(3, 6, 6)],
        scratch_shapes=[
            VMEM((16, 128), F32),
            VMEM((16, 128), F32),
            VMEM((192, 384), F32),
        ],
        compiler_params=SMALL,
        name="finish",
    )(*args)


def local(
    fine_now, fine_prev, fine_mu, fine_coef, coarse_now, coarse_prev, coarse_mu, coarse_coef, src_cell, src_moment,
):
    rows = make_rows(fine_now, coarse_now, coarse_mu, src_moment)
    gathered = lax.all_to_all(rows.reshape(NX * NY, 1, 128), AX, 0, 0, tiled=True).reshape(NX * NY, 128)
    own, xa, xb, ya, yb = pack_halos(fine_now, coarse_now, coarse_mu)
    ya, yb = swapped(ya, "gy", 0), swapped(yb, "gy", 1)
    xb, xa = swapped(xb, "gx", 1), swapped(xa, "gx", 0)
    found = find_sources(src_cell)
    base = base_step(
        fine_now, fine_prev, fine_mu, fine_coef, coarse_now, coarse_prev, coarse_mu, coarse_coef, ya, yb
    )
    return finish(
        *found, *base, fine_mu, fine_coef, coarse_mu, coarse_coef, own, ya, yb, xb, xa, gathered
    )


def solution(mesh):
    in_specs = (
        P(None, "gx", "gy", None),
        P(None, "gx", "gy", None),
        P("gx", "gy", None),
        P("gx", "gy", None),
        P(None, "gx", "gy", None),
        P(None, "gx", "gy", None),
        P("gx", "gy", None),
        P("gx", "gy", None),
        P(),
        P(None, ("gx", "gy")),
    )
    out_specs = (P(None, "gx", "gy", None), P(None, "gx", "gy", None), P(None, "gx", "gy"))
    return jax.shard_map(local, mesh=mesh, in_specs=in_specs, out_specs=out_specs, check_vma=False)
```

```python
import jax
import jax.numpy as jnp
from jax import lax
from jax.experimental import pallas as pl
from jax.experimental.pallas import tpu as pltpu
from jax.sharding import PartitionSpec as P

ITERS = 3
NX, NY = 32, 16
FIRST_LIMIT = 60 * 1024 * 1024
AX = ("gx", "gy")
ROWS_YA = 124
ROWS_YB = 136
GROW = 108
ROWS_XA = 120
ROWS_XB = 128
VMEM = pltpu.VMEM
F32 = jnp.float32


def vspec(n):
    return [pl.BlockSpec(memory_space=VMEM)] * n


def lane_iota(shape):
    return lax.broadcasted_iota(jnp.int32, shape, len(shape) - 1)


def row_iota(shape):
    return lax.broadcasted_iota(jnp.int32, shape, 0)


def interface_piece(fine, coarse, mu, a_s, g_s, ready):
    lane = lane_iota((1, 128))
    b = jnp.zeros((6, 128), F32)
    ready(3)
    ready(4)
    for i in range(6):
        for c in range(3):
            col = 2.0 * coarse[c, i, :, 0:1] - coarse[c, i, :, 1:2]
            b = b + jnp.where(lane == c * 16 + 3 + i, col, 0.0)
        inv = 1.0 / (0.6 + mu[i, :, 0:1])
        b = b + jnp.where(lane == 48 + 3 + i, inv, 0.0)
    acc = jnp.zeros((12, 128), F32)
    for c in range(3):
        ready(c)
        for x in range(12):
            at = c * 16 + 3 + x // 2
            if x % 2 == 0:
                w = jnp.where(lane == at, 0.5, 0.0)
            else:
                w = jnp.where((lane == at) | (lane == at + 1), 0.25, 0.0)
            acc = acc + fine[c, x, :, 126:127] * w
    a_s[...] = jnp.zeros((24, 128), F32)
    a_s[1:13, :] = acc
    g_s[...] = jnp.zeros((16, 128), F32)
    for j in range(7):
        g_s[3 + j : 4 + j, :] = (
            0.25 * a_s[2 * j : 2 * j + 1, :]
            + 0.5 * a_s[2 * j + 1 : 2 * j + 2, :]
            + 0.25 * a_s[2 * j + 2 : 2 * j + 3, :]
        )
    g_s[3:9, :] = g_s[3:9, :] + b


def rows_kernel(fine_hbm, coarse_hbm, mu_hbm, mom_hbm, rows, a_s, g_s, fine, coarse, mu, mom, sems):
    copies = [pltpu.make_async_copy(fine_hbm.at[c], fine.at[c], sems.at[c]) for c in range(3)]
    copies.append(pltpu.make_async_copy(coarse_hbm, coarse, sems.at[3]))
    copies.append(pltpu.make_async_copy(mu_hbm, mu, sems.at[4]))
    copies.append(pltpu.make_async_copy(mom_hbm, mom, sems.at[5]))
    for n in (0, 1, 2, 5, 3, 4):
        copies[n].start()
    lane = lane_iota((1, 128))
    lanes = lane_iota((6, 128))
    want = 8 * row_iota((6, 128)) + 64
    t = jnp.zeros((6, 128), F32)
    copies[5].wait()
    for j in range(8):
        t = t + jnp.where(lanes == want + j, mom[:, j : j + 1], 0.0)
    row = jnp.sum(t, axis=0, keepdims=True)
    rows[...] = jnp.broadcast_to(row, rows.shape)
    interface_piece(fine, coarse, mu, a_s, g_s, lambda n: copies[n].wait())
    ix = lax.axis_index("gx")
    iy = lax.axis_index("gy")
    for a in (1, -1):
        for b in (1, -1):
            from_x, from_y = 6 if a > 0 else 3, 6 if b > 0 else 3
            corner = row
            for j in range(4):
                line = pltpu.roll(g_s[from_y + j : from_y + j + 1, :], (128 + 4 * j - from_x) % 128, 1)
                corner = corner + jnp.where((lane < 64) & ((lane & 15) // 4 == j), line, 0.0)

            @pl.when(inside(ix + a, iy + b))
            def _():
                rows[pl.ds((ix + a) * NY + iy + b, 1), :] = corner


def pack_kernel(fine, coarse, mu, own, xa, xb, ya, yb, a_s, g_s):
    interface_piece(fine, coarse, mu, a_s, g_s, lambda n: None)
    g = g_s[...]
    own[...] = g
    odd_x = (lax.axis_index("gx") & 1) == 1
    odd_y = (lax.axis_index("gy") & 1) == 1

    def put(refs, odd, rows, up, down):
        one, two = refs
        one[rows, :] = jnp.where(odd, down, up)
        two[rows, :] = jnp.where(odd, up, down)

    for c in range(3):
        for j in range(2):
            at = 12 * (2 * c + j)
            put((xa, xb), odd_x, slice(at, at + 12), fine[c, 10 + j], fine[c, j])
            at = 72 + 6 * (2 * c + j)
            put((xa, xb), odd_x, slice(at, at + 6), coarse[c, 4 + j], coarse[c, j])
        for x in range(12):
            at = 2 * (12 * c + x)
            put((ya, yb), odd_y, slice(at, at + 2), fine[c, x, 10:12, :], fine[c, x, 0:2, :])
        for x in range(6):
            at = 72 + 2 * (6 * c + x)
            put((ya, yb), odd_y, slice(at, at + 2), coarse[c, x, 4:6, :], coarse[c, x, 0:2, :])
    place = lane_iota((16, 128)) & 15
    row = row_iota((16, 128))
    here = slice(GROW, GROW + 16)
    up = jnp.where(place < 4, pltpu.roll(g, 128 - 6, 1), 0.0)
    down = jnp.where((place >= 9) & (place < 13), pltpu.roll(g, 6, 1), 0.0)
    put((xa, xb), odd_x, slice(GROW, GROW + 8), up[3:11, :], down[3:11, :])
    up = jnp.where(row < 4, pltpu.roll(g, 16 - 6, 0), 0.0)
    down = jnp.where((row >= 9) & (row < 13), pltpu.roll(g, 6, 0), 0.0)
    put((ya, yb), odd_y, here, up, down)
    xa[GROW + 8 : ROWS_XA, :] = jnp.zeros((ROWS_XA - GROW - 8, 128), F32)
    yb[GROW + 16 : ROWS_YB, :] = jnp.zeros((ROWS_YB - GROW - 16, 128), F32)
    xb[GROW + 8 : ROWS_XB, :] = jnp.zeros((ROWS_XB - GROW - 8, 128), F32)


def inside(x, y):
    return (x >= 0) & (x < NX) & (y >= 0) & (y < NY)


def lower(rows, one, two, odd):
    return jnp.where(odd, one[rows, :], two[rows, :])


def upper(rows, one, two, odd):
    return jnp.where(odd, two[rows, :], one[rows, :])


def base_kernel(fine, prev, mu, coef, coarse, cprev, cmu, ccoef, ya, yb, base, cbase, yf, yc):
    odd_y = (lax.axis_index("gy") & 1) == 1

    def terms(field, pad, c, x, at, size, edge):
        u = field[c, x]
        k = size * c + x
        rows = slice(at + 2 * k, at + 2 * k + 2)
        pad[k, 0:2, :] = lower(rows, ya, yb, odd_y)
        pad[k, 2 : size + 2, :] = u
        pad[k, size + 2 : size + 4, :] = upper(rows, ya, yb, odd_y)
        near = pad[k, 1 : size + 1, :] + pad[k, 3 : size + 3, :]
        far = pad[k, 0:size, :] + pad[k, 4 : size + 4, :]
        for d in (-1, 1):
            if 0 <= x + d < size:
                near = near + field[c, x + d]
            if 0 <= x + 2 * d < size:
                far = far + field[c, x + 2 * d]
        below = pltpu.roll(u, 127, 1)
        above = pltpu.roll(u, 1, 1)
        lane = lane_iota((size, 128))
        above = jnp.where(lane == 0, below if edge else 0.0, above)
        below = jnp.where(lane == 127, 0.0, below)
        return u, (16.0 * near - far) * (1.0 / 12.0) - 7.0 * u + above + below

    for x in range(12):
        cm = coef[x] * mu[x]
        for c in range(3):
            u, t = terms(fine, yf, c, x, 0, 12, True)
            base[c, x] = 2.0 * u - prev[c, x] + cm * t
    for x in range(6):
        cm = 0.25 * (ccoef[x] * cmu[x])
        for c in range(3):
            u, t = terms(coarse, yc, c, x, 72, 6, False)
            cbase[c, x] = 2.0 * u - cprev[c, x] + cm * t


def finish_kernel(
    pick, rank, first, second, base_lane, here, step, spread,
    base, cbase, mu, coef, cmu, ccoef, own, ya, yb, xb, xa, rows,
    fnext, cnext, ghost, g_s, f_s, force,
):
    lane = lane_iota((16, 128))
    line = lane_iota((1, 128))
    force[...] = source_force(rows, pick[...], base_lane[...], here[...], step[...], spread[...])
    g_s[...] = own[...] + ya[GROW : GROW + 16, :] + yb[GROW : GROW + 16, :]
    g_s[3:11, :] = g_s[3:11, :] + xa[GROW : GROW + 8, :] + xb[GROW : GROW + 8, :]
    ix = lax.axis_index("gx")
    iy = lax.axis_index("gy")
    for a in (1, -1):
        for b in (1, -1):
            ok = inside(ix + a, iy + b)
            at = jnp.where(ok, (ix + a) * NY + iy + b, 0)
            corner = jnp.where(ok, rows[pl.ds(at, 1), :], 0.0)
            to_x, to_y = 9 if a > 0 else 0, 9 if b > 0 else 0
            keep = (line < 64) & ((line & 15) >= to_x) & ((line & 15) < to_x + 4)
            for j in range(4):
                part = jnp.where(keep, pltpu.roll(corner, (128 + to_x - 4 * j) % 128, 1), 0.0)
                g_s[to_y + j : to_y + j + 1, :] = g_s[to_y + j : to_y + j + 1, :] + part
    g_in = g_s[...]
    only = jnp.where((lane >= 48) & (lane < 64), g_in, 0.0)
    inv = pltpu.roll(only, 128 - 48, 1) + pltpu.roll(only, 128 - 32, 1) + pltpu.roll(only, 128 - 16, 1)
    g = inv * g_in
    for _ in range(ITERS):
        t = (pltpu.roll(g, 1, 1) + pltpu.roll(g, 127, 1) + 6.0 * g) * 0.125
        t = (pltpu.roll(t, 1, 0) + pltpu.roll(t, 15, 0) + 6.0 * t) * 0.125
        g = inv * (g_in + t)
    g_s[...] = g
    turned = g.T
    for c in range(3):
        ghost[c] = turned[16 * c + 3 : 16 * c + 9, 3:9]
    for j in range(6):
        low = g_s[3 + j : 4 + j, :]
        f_s[2 * j : 2 * j + 1, :] = low
        f_s[2 * j + 1 : 2 * j + 2, :] = 0.5 * (low + g_s[4 + j : 5 + j, :])
    even = f_s[0:12, :]
    odd = 0.5 * (even + pltpu.roll(even, 127, 1))
    coarse_g = g_s[3:9, :]
    def more(number, carry):
        force[...] = force[...] + source_force(rows, *matrices(*columns(number, rank, first, second)))
        return carry

    found = jnp.max(rank[...]).astype(jnp.int32) + 1
    lax.fori_loop(1, (found + K - 1) // K, more, 0)

    odd_x = (ix & 1) == 1

    def halo(c, x, at, size):
        rows = [slice(n, n + size) for n in (at + 2 * size * c, at + 2 * size * c + size)]
        low = [lower(n, xa, xb, odd_x) for n in rows]
        high = [upper(n, xa, xb, odd_x) for n in rows]
        if x == 0:
            return (16.0 * low[1] - low[0]) * (1.0 / 12.0)
        if x == 1:
            return low[1] * (-1.0 / 12.0)
        if x == size - 2:
            return high[0] * (-1.0 / 12.0)
        if x == size - 1:
            return (16.0 * high[0] - high[1]) * (1.0 / 12.0)
        return 0.0

    lane12 = lane_iota((12, 128))
    for x in range(12):
        cm = coef[x] * mu[x]
        for c in range(3):
            at = 16 * c + 3 + x // 2
            edge = (even if x % 2 == 0 else odd)[:, at : at + 1]
            extra = halo(c, x, 0, 12) + jnp.where(lane12 == 127, edge, 0.0)
            push = coef[x] * force[16 * x : 16 * x + 12, 128 * c : 128 * (c + 1)]
            fnext[c, x] = base[c, x] + cm * extra + push
    lane6 = lane_iota((6, 128))
    for x in range(6):
        cm = 0.25 * (ccoef[x] * cmu[x])
        for c in range(3):
            at = 16 * c + 3 + x
            extra = halo(c, x, 72, 6) + jnp.where(lane6 == 0, coarse_g[:, at : at + 1], 0.0)
            cnext[c, x] = cbase[c, x] + cm * extra


K = 24
PART = 80


def matrices(first, second):
    lanes = lane_iota((K, 128))
    base_lane = jnp.broadcast_to(64 + (first & 7), (K, 128))
    z = second & 127
    live = first >= 0
    here = jnp.where((lanes == z) & live, 1.0, 0.0)
    step = jnp.where((lanes == z + 1) & live, 1.0, 0.0) - jnp.where((lanes == z - 1) & live, 1.0, 0.0)
    lx = (second >> 11) - 1
    ly = ((second >> 7) & 15) - 1
    at = 16 * lx + ly
    place = lane_iota((K, 192))
    along_x = jnp.where(place == at + 16, 1.0, 0.0) - jnp.where(place == at - 16, 1.0, 0.0)
    along_y = jnp.where(place == at + 1, 1.0, 0.0) - jnp.where(place == at - 1, 1.0, 0.0)
    centre = jnp.where(place == at, 1.0, 0.0)
    part = [along_x, along_y, centre, jnp.zeros((8, 192), F32)]
    spread = jnp.concatenate(part * 3 + [jnp.zeros((256 - 3 * PART, 192), F32)], axis=0)
    pick = jnp.where(lane_iota((K, NX * NY)) == first >> 3, 1.0, 0.0)
    return pick, base_lane, here, step, spread.T.astype(jnp.bfloat16)


def columns(number, rank, first, second):
    want = (row_iota((K, 128)) + number * K).astype(F32)
    one = jnp.zeros((K, 128), F32)
    two = jnp.zeros((K, 128), F32)
    for r in range(32):
        same = rank[r : r + 1, :] == want
        one = one + jnp.where(same, first[r : r + 1, :], 0.0)
        two = two + jnp.where(same, second[r : r + 1, :], 0.0)
    one = jnp.sum(one, axis=1, keepdims=True).astype(jnp.int32) - 1
    two = jnp.sum(two, axis=1, keepdims=True).astype(jnp.int32)
    return one, two


def find_kernel(cells, pick, rank, first, second, base_lane, here, step, spread, cell_s):
    for r in range(32):
        for n in range(3):
            cell_s[n, r : r + 1, :] = cells[n : n + 1, 128 * r : 128 * (r + 1)]
    lx = cell_s[0] - 12 * lax.axis_index("gx")
    ly = cell_s[1] - 12 * lax.axis_index("gy")
    hit = jnp.where((lx >= -1) & (lx <= 12) & (ly >= -1) & (ly <= 12), 1.0, 0.0)
    block = (32, 128)
    first[...] = (lane_iota(block) + 128 * row_iota(block) + 1).astype(F32)
    second[...] = (((lx + 1) << 11) + ((ly + 1) << 7) + cell_s[2]).astype(F32)
    square = (128, 128)
    before = jnp.where(row_iota(square) < lane_iota(square), 1.0, 0.0)
    within = jnp.dot(hit, before, preferred_element_type=F32)
    total = jnp.dot(hit, jnp.ones(square, F32), preferred_element_type=F32)
    above = jnp.where(lane_iota((32, 32)) < row_iota((32, 32)), 1.0, 0.0)
    earlier = jnp.dot(above, total, preferred_element_type=F32)
    rank[...] = jnp.where(hit > 0.0, within + earlier, -1.0)
    one, two = columns(0, rank, first, second)
    pick[...], base_lane[...], here[...], step[...], spread[...] = matrices(one, two)


def exact_parts(x):
    parts = []
    for _ in range(3):
        parts.append(x.astype(jnp.bfloat16))
        x = x - parts[-1].astype(F32)
    return parts


def source_force(rows, pick, base_lane, here, step, spread):
    line = jnp.dot(
        pick.astype(jnp.bfloat16), jnp.concatenate(exact_parts(rows[...]), axis=1), preferred_element_type=F32
    )
    line = line[:, 0:128] + line[:, 128:256] + line[:, 256:384]
    lanes = lane_iota((K, 128)) - base_lane
    m = [0.5 * jnp.sum(jnp.where(lanes == 8 * i, line, 0.0), axis=1, keepdims=True) for i in range(6)]
    zeros = jnp.zeros((8, 128), F32)
    wide = []
    for a, b, c in ((0, 3, 4), (3, 1, 5), (4, 5, 2)):
        wide.append(jnp.concatenate([m[a] * here, m[b] * here, m[c] * step, zeros], axis=0))
    parts = exact_parts(jnp.concatenate(wide, axis=1))
    parts.append(jnp.zeros((256 - 3 * PART, 384), jnp.bfloat16))
    return jnp.dot(spread, jnp.concatenate(parts, axis=0), preferred_element_type=F32)


def shape(*dims):
    return jax.ShapeDtypeStruct(dims, F32)


def swapped(x, axis, first):
    pairs = [(i, i + 1) for i in range(first, lax.axis_size(axis) - 1, 2)]
    return lax.ppermute(x, axis, pairs + [(j, i) for i, j in pairs])


SMALL = pltpu.CompilerParams(vmem_limit_bytes=32 * 1024 * 1024)
PIECE = [VMEM((24, 128), F32), VMEM((16, 128), F32)]


def make_rows(fine_now, coarse_now, coarse_mu, src_moment):
    return pl.pallas_call(
        rows_kernel,
        in_specs=[pl.BlockSpec(memory_space=pltpu.HBM)] * 4,
        out_specs=vspec(1)[0],
        out_shape=shape(NX * NY, 128),
        scratch_shapes=PIECE
        + [
            VMEM((3, 12, 12, 128), F32),
            VMEM((3, 6, 6, 128), F32),
            VMEM((6, 6, 128), F32),
            VMEM((6, 8), F32),
            pltpu.SemaphoreType.DMA((6,)),
        ],
        compiler_params=pltpu.CompilerParams(vmem_limit_bytes=FIRST_LIMIT),
        name="make_rows",
    )(fine_now, coarse_now, coarse_mu, src_moment)


def pack_halos(fine_now, coarse_now, coarse_mu):
    return pl.pallas_call(
        pack_kernel,
        in_specs=vspec(3),
        out_specs=vspec(5),
        out_shape=[shape(16, 128)] + [shape(n, 128) for n in (ROWS_XA, ROWS_XB, ROWS_YA, ROWS_YB)],
        scratch_shapes=PIECE,
        compiler_params=SMALL,
        name="pack_halos",
    )(fine_now, coarse_now, coarse_mu)


def find_sources(src_cell):
    return pl.pallas_call(
        find_kernel,
        in_specs=vspec(1),
        out_specs=vspec(8),
        out_shape=[
            shape(K, NX * NY),
            shape(32, 128), shape(32, 128), shape(32, 128),
            jax.ShapeDtypeStruct((K, 128), jnp.int32),
            shape(K, 128), shape(K, 128), jax.ShapeDtypeStruct((192, 256), jnp.bfloat16),
        ],
        scratch_shapes=[VMEM((3, 32, 128), jnp.int32)],
        compiler_params=SMALL,
        name="find_sources",
    )(src_cell)


def base_step(*args):
    return pl.pallas_call(
        base_kernel,
        in_specs=vspec(10),
        out_specs=vspec(2),
        out_shape=[shape(3, 12, 12, 128), shape(3, 6, 6, 128)],
        scratch_shapes=[VMEM((36, 16, 128), F32), VMEM((18, 16, 128), F32)],
        compiler_params=SMALL,
        name="base_step",
    )(*args)


def finish(*args):
    return pl.pallas_call(
        finish_kernel,
        in_specs=vspec(20),
        out_specs=vspec(3),
        out_shape=[shape(3, 12, 12, 128), shape(3, 6, 6, 128), shape(3, 6, 6)],
        scratch_shapes=[
            VMEM((16, 128), F32),
            VMEM((16, 128), F32),
            VMEM((192, 384), F32),
        ],
        compiler_params=SMALL,
        name="finish",
    )(*args)


def local(
    fine_now, fine_prev, fine_mu, fine_coef, coarse_now, coarse_prev, coarse_mu, coarse_coef, src_cell, src_moment,
):
    rows = make_rows(fine_now, coarse_now, coarse_mu, src_moment)
    gathered = lax.all_to_all(rows.reshape(NX * NY, 1, 128), AX, 0, 0, tiled=True).reshape(NX * NY, 128)
    own, xa, xb, ya, yb = pack_halos(fine_now, coarse_now, coarse_mu)
    ya, yb = swapped(ya, "gy", 0), swapped(yb, "gy", 1)
    xb, xa = swapped(xb, "gx", 1), swapped(xa, "gx", 0)
    found = find_sources(src_cell)
    base = base_step(
        fine_now, fine_prev, fine_mu, fine_coef, coarse_now, coarse_prev, coarse_mu, coarse_coef, ya, yb
    )
    return finish(
        *found, *base, fine_mu, fine_coef, coarse_mu, coarse_coef, own, ya, yb, xb, xa, gathered
    )


def solution(mesh):
    in_specs = (
        P(None, "gx", "gy", None),
        P(None, "gx", "gy", None),
        P("gx", "gy", None),
        P("gx", "gy", None),
        P(None, "gx", "gy", None),
        P(None, "gx", "gy", None),
        P("gx", "gy", None),
        P("gx", "gy", None),
        P(),
        P(None, ("gx", "gy")),
    )
    out_specs = (P(None, "gx", "gy", None), P(None, "gx", "gy", None), P(None, "gx", "gy"))
    return jax.shard_map(local, mesh=mesh, in_specs=in_specs, out_specs=out_specs, check_vma=False)
```
